256 devices in a mesh: ctx: 256 (over z, y, x, core).
Axes of the slice: x: 4, y: 4, z: 8, core: 2. Of those that a mesh axis runs over, the one named last changes fastest.
Arguments:
- queries: bfloat16 [131072, 1024], P('ctx'), may hold values from -6.5 to 6.5
- keys: bfloat16 [131072, 128], P('ctx'), may hold values from -4 to 4
- values: bfloat16 [131072, 128], P('ctx'), may hold values from -6 to 6
- doc_ids: int32 [131072], P('ctx'), may hold values from 0 to 63, never falling along the last dimension, each value on 1 to 4096 neighbouring positions
Outputs:
- attended: bfloat16 [131072, 1024], P('ctx')
The draws below stay inside these ranges and needn't reach their ends.
All inputs are finite; a program needn't handle non-finite values.
Results may differ from the reference program's by a relative error of at most 0.024.
Values may be sent and summed in bfloat16 or wider, within the bound.
No kernel may reach another device: no remote copies, remote signals or barrier semaphores. Data moves between devices by JAX's collectives and lax.ppermute only.
A program may use at most 64 MiB of HBM per device.

```python
import math
import jax
import jax.numpy as jnp
import numpy as np
from jax import lax

TOK_DEV = 512
HEADS = 8
HEAD_DIM = 128
HOPS = 4
TOKENS = 131072
SEGS = 64


def draw_keys(key, part):
    key = jax.random.fold_in(key, 1)
    result = jnp.clip(jax.random.normal(key, (TOKENS, HEAD_DIM), jnp.float32), -4.0, 4.0)
    return result.astype(jnp.bfloat16)


def draw_queries(key, part):
    key = jax.random.fold_in(key, 2)
    result = jnp.clip(jax.random.normal(key, (TOKENS, HEADS, HEAD_DIM), jnp.float32), -4.0, 4.0)
    return result.reshape(TOKENS, HEADS * HEAD_DIM).astype(jnp.bfloat16)


def level_of(stream_key, extent, cuts, low, largest):
    loudness = 1.0
    for axis_at, shards_of in cuts:
        steps = jax.random.uniform(jax.random.fold_in(jax.random.fold_in(stream_key, 6), axis_at), (shards_of,), jnp.float32, low / len(cuts), largest / len(cuts))
        loudness = loudness * jnp.repeat(jnp.exp(steps), extent[axis_at] // shards_of).reshape((-1,) + (1,) * (len(extent) - 1 - axis_at))
    return loudness


def profile(number_of, total, reach, slope):
    portions = [(1 << 20) // math.isqrt(standing ** slope) + 1 for standing in range(2, number_of + 1)]
    rest, counts = total - reach - (number_of - 1), [1] * (number_of - 1)
    while rest > 0:
        movable = [i for i in range(number_of - 1) if counts[i] < reach]
        mass, remaining = sum([portions[i] for i in movable]), rest
        for i in movable:
            extra = min(reach - counts[i], max(1, remaining * portions[i] // mass), rest)
            counts[i] = counts[i] + extra
            rest = rest - extra
    return np.array([reach] + counts)


def uneven(own_key, number_of, total, limit, lean):
    if number_of == 2:
        one = jax.random.randint(own_key, (), max(1, total - limit), min(limit, total - 1) + 1)
        return jnp.stack([one, total - one])
    sizes = jnp.asarray(profile(number_of, total, limit, lean), jnp.int32)
    pairs = (number_of - 1) // 2
    donor, taker = sizes[1:1 + 2 * pairs:2], sizes[2:2 + 2 * pairs:2]
    slack = jnp.minimum(donor - 1, limit - taker)
    shifted = jax.random.randint(jax.random.fold_in(own_key, 1), (pairs,), 0, 1 << 20) % (slack + 1)
    sizes = sizes.at[1:1 + 2 * pairs:2].set(donor - shifted).at[2:2 + 2 * pairs:2].set(taker + shifted)
    return sizes[jax.random.permutation(jax.random.fold_in(own_key, 2), number_of)]


def scatter_about(stream_key, extent, scale, most, cuts=(), kind=jnp.bfloat16):
    entries = scale * jax.random.normal(stream_key, extent, jnp.float32)
    if cuts:
        entries = entries * level_of(stream_key, extent, cuts, -0.22, 0.18)
    return jnp.clip(entries, -most, most).astype(kind)


def setup_inputs(seed: int = 0) -> dict:
    seeds = jax.random.split(jax.random.key(seed), 5)
    queries = draw_queries(jax.random.fold_in(seeds[4], 71), 0)
    keys = draw_keys(jax.random.fold_in(seeds[4], 71), 0)
    values = scatter_about(seeds[2], (TOKENS, HEAD_DIM), 1.0, 6.0, ((0, 256),))
    doc_ids = jnp.searchsorted(jnp.cumsum(uneven(seeds[3], SEGS, TOKENS, 8 * TOK_DEV, 2)), jnp.arange(TOKENS), side="right").astype(jnp.int32)
    return dict(queries=queries, keys=keys, values=values, doc_ids=doc_ids)


def block_partial(query, query_docs, block_keys, block_values, key_docs, offset, rows):
    heads = query.shape[1] // block_keys.shape[1]
    depth = block_keys.shape[1]
    query_three = query.reshape(rows, heads, depth)
    scores = jnp.einsum("phd,jd->hpj", query_three.astype(jnp.float32), block_keys.astype(jnp.float32)) * (1.0 / (depth ** 0.5))
    rel = offset + jnp.arange(rows, dtype=jnp.int32)[None, :] - jnp.arange(rows, dtype=jnp.int32)[:, None]
    allowed = (rel <= 0) & (rel > -HOPS * rows) & (key_docs[None, :] == query_docs[:, None])
    masked = jnp.where(allowed[None], scores, jnp.float32(-1e30))
    top = jnp.max(masked, axis=2)
    expo = jnp.where(allowed[None], jnp.exp(masked - top[:, :, None]), jnp.float32(0.0))
    total = jnp.sum(expo, axis=2)
    weight = expo.astype(jnp.bfloat16)
    out = jnp.einsum("hpj,jd->phd", weight.astype(jnp.float32), block_values.astype(jnp.float32)).astype(jnp.bfloat16)
    return out, top.T, total.T


def merge_parts(parts, rows):
    best = parts[0][1]
    for part in parts[1:]:
        best = jnp.maximum(best, part[1])
    numer = jnp.zeros(parts[0][0].shape, jnp.float32)
    denom = jnp.zeros(best.shape, jnp.float32)
    for out, top, total in parts:
        factor = jnp.exp(top - best)
        numer = numer + factor[:, :, None] * out.astype(jnp.float32)
        denom = denom + factor * total
    return (numer / denom[:, :, None]).reshape(rows, -1).astype(jnp.bfloat16)


def reference(queries, keys, values, doc_ids):
    rows = TOK_DEV
    blocks = queries.shape[0] // rows
    pad = HOPS * rows
    keys_pad = jnp.concatenate([jnp.zeros((pad, keys.shape[1]), keys.dtype), keys], axis=0)
    values_pad = jnp.concatenate([jnp.zeros((pad, values.shape[1]), values.dtype), values], axis=0)
    docs_pad = jnp.concatenate([jnp.full((pad,), -1, jnp.int32), doc_ids.astype(jnp.int32)], axis=0)

    def one_block(index):
        start = (index * rows).astype(jnp.int32)
        query = lax.dynamic_slice_in_dim(queries, start, rows, 0)
        query_docs = lax.dynamic_slice_in_dim(doc_ids, start, rows, 0)
        parts = []
        for step in range(HOPS + 1):
            kstart = (start + step * rows).astype(jnp.int32)
            parts.append(block_partial(query, query_docs,
                                       lax.dynamic_slice_in_dim(keys_pad, kstart, rows, 0),
                                       lax.dynamic_slice_in_dim(values_pad, kstart, rows, 0),
                                       lax.dynamic_slice_in_dim(docs_pad, kstart, rows, 0),
                                       (step - HOPS) * rows, rows))
        return merge_parts(parts, rows)

    result = lax.map(one_block, jnp.arange(blocks, dtype=jnp.int32))
    return result.reshape(queries.shape[0], -1)
```

```python
import jax
import jax.numpy as jnp
from jax import lax
from jax.experimental import pallas as pl
from jax.experimental.pallas import tpu as pltpu
from jax.sharding import PartitionSpec as P

ROWS = 512
HALF = 256
DEPTH = 128
HEADS = 8
SCALE = 1.4426950408889634 / DEPTH**0.5
NEG = -1e30
LOW, HIGH = 2.0**-60, 2.0**100
VM = pl.BlockSpec(memory_space=pltpu.VMEM)
BLOCK = (ROWS + 16, HALF)
QT = (HEADS * DEPTH, ROWS)
SUMS = (HEADS * 8, ROWS)
F32 = jnp.float32
BF16 = jnp.bfloat16


def call(body, out, aliases=None, flops=0, exps=0, scratch=()):
    return pl.pallas_call(
        body,
        out_shape=out,
        out_specs=jax.tree.map(lambda _: VM, out),
        scratch_shapes=scratch,
        input_output_aliases=aliases or {},
        cost_estimate=pl.CostEstimate(
            flops=flops, bytes_accessed=1 << 20, transcendentals=exps
        ),
        compiler_params=pltpu.CompilerParams(vmem_limit_bytes=16 << 20),
    )


def pack(k_ref, v_ref, d_ref, o_ref):
    o_ref[0:HALF, 0:DEPTH] = k_ref[0:HALF, :]
    o_ref[0:HALF, DEPTH:HALF] = k_ref[HALF:ROWS, :]
    vt = v_ref[...].astype(F32).T.astype(BF16)
    o_ref[HALF : HALF + DEPTH, :] = vt[:, 0:HALF]
    o_ref[HALF + DEPTH : ROWS, :] = vt[:, HALF:ROWS]
    d = (d_ref[...] + 1).astype(F32)
    o_ref[ROWS : ROWS + 16, :] = jnp.concatenate(
        [d, jnp.zeros((14, HALF), F32)], axis=0
    ).astype(BF16)


def keys(ref, half):
    return ref[0:HALF, half * DEPTH : (half + 1) * DEPTH]


def values(ref, half):
    return ref[HALF + half * DEPTH : HALF + (half + 1) * DEPTH, :]


def docs(ref, half):
    return ref[ROWS : ROWS + 16, :].astype(F32)[half : half + 1, :]


def column(row):
    return jnp.broadcast_to(row, (DEPTH, row.shape[1])).T


def widen(col, lanes):
    return jnp.concatenate([col] * (lanes // DEPTH), axis=1)


def first_doc(own_ref):
    return docs(own_ref, 0)[:, 0:1]


def row_mask(own_ref):
    both = jnp.concatenate([docs(own_ref, 0), docs(own_ref, 1)], axis=1)
    return jnp.where(both == first_doc(own_ref), 1.0, 0.0)


def key_match(own_ref, ref, half):
    return jnp.where(docs(ref, half) == first_doc(own_ref), 1.0, 0.0)


def key_bias(own_ref, ref, half):
    return column((1.0 - key_match(own_ref, ref, half)) * NEG)


def dot(a, b):
    return jnp.dot(a, b, preferred_element_type=F32)


def fold(e):
    return jnp.sum(e.reshape(e.shape[0] // 8, 8, e.shape[1]), axis=0)


def tile(k, vt, qt, bias):
    e = jnp.exp2(dot(k, qt) * SCALE + bias)
    return dot(vt, e.astype(BF16)), fold(e)


def triangle(strict):
    key = lax.broadcasted_iota(jnp.int32, (HALF, HALF), 0)
    row = lax.broadcasted_iota(jnp.int32, (HALF, HALF), 1)
    keep = key > row if strict else key <= row
    return jnp.where(keep, 0.0, NEG)


def own_block(q_ref, own_ref, e0_ref, qt_ref, acc_ref, sum_ref):
    rows = [docs(own_ref, 0), docs(own_ref, 1)]
    cols = [widen(column(r), HALF) for r in rows]
    apart = lambda k, r: jnp.where(cols[k] == rows[r], 0.0, NEG)
    tri = triangle(False)
    bias = {(0, 0): apart(0, 0) + tri, (0, 1): apart(0, 1), (1, 1): apart(1, 1) + tri}
    for h in range(HEADS):
        hs = slice(h * DEPTH, (h + 1) * DEPTH)
        ss = slice(h * 8, (h + 1) * 8)
        qt = q_ref[:, hs].astype(F32).T.astype(BF16)
        qt_ref[hs, :] = qt
        for r in range(2):
            cs = slice(r * HALF, (r + 1) * HALF)
            o = t = None
            for k in range(r + 1):
                oo, tt = tile(keys(own_ref, k), values(own_ref, k), qt[:, cs], bias[k, r])
                o, t = (oo, tt) if o is None else (o + oo, t + tt)
            acc_ref[hs, cs] = o
            sum_ref[ss, cs] = t

    @pl.when(any_seen(own_ref, e0_ref))
    def _():
        put = keeper(acc_ref, sum_ref)
        full_heads(own_ref, e0_ref, qt_ref, acc_ref, sum_ref, put)


def any_seen(own_ref, ref):
    seen = key_match(own_ref, ref, 0) + key_match(own_ref, ref, 1)
    return jnp.max(seen) > 0.5


def full_heads(own_ref, ref, qt_ref, acc_in, sum_in, put):
    mask = row_mask(own_ref)
    bias = [widen(key_bias(own_ref, ref, k), ROWS) for k in range(2)]
    for h in range(HEADS):
        hs = slice(h * DEPTH, (h + 1) * DEPTH)
        ss = slice(h * 8, (h + 1) * 8)
        qt = qt_ref[hs, :]
        o0, t0 = tile(keys(ref, 0), values(ref, 0), qt, bias[0])
        o1, t1 = tile(keys(ref, 1), values(ref, 1), qt, bias[1])
        put(h, acc_in[hs, :] + (o0 + o1) * mask, sum_in[ss, :] + (t0 + t1) * mask)


def keeper(acc_ref, sum_ref):
    def put(h, acc, sums):
        acc_ref[h * DEPTH : (h + 1) * DEPTH, :] = acc
        sum_ref[h * 8 : (h + 1) * 8, :] = sums

    return put


def full_block(own_ref, ref, qt_ref, acc_in, sum_in, acc_ref, sum_ref):
    seen = any_seen(own_ref, ref)

    @pl.when(seen)
    def _():
        full_heads(own_ref, ref, qt_ref, acc_in, sum_in, keeper(acc_ref, sum_ref))

    @pl.when(jnp.logical_not(seen))
    def _():
        acc_ref[...] = acc_in[...]
        sum_ref[...] = sum_in[...]


def far_block(own_ref, ref, qt_ref, acc_in, sum_in, acc_ref, sum_ref):
    seen = any_seen(own_ref, ref)

    @pl.when(jnp.logical_not(seen))
    def _():
        acc_ref[...] = acc_in[...]
        sum_ref[...] = sum_in[...]

    @pl.when(seen)
    def _():
        mask = row_mask(own_ref)
        cols = [widen(key_bias(own_ref, ref, k), HALF) for k in range(2)]
        tri = triangle(True)
        bias = {(0, 0): cols[0] + tri, (1, 0): cols[1], (1, 1): cols[1] + tri}
        for h in range(HEADS):
            hs = slice(h * DEPTH, (h + 1) * DEPTH)
            ss = slice(h * 8, (h + 1) * 8)
            for r in range(2):
                cs = slice(r * HALF, (r + 1) * HALF)
                qt = qt_ref[hs, cs]
                o = t = None
                for k in range(r, 2):
                    oo, tt = tile(keys(ref, k), values(ref, k), qt, bias[k, r])
                    o, t = (oo, tt) if o is None else (o + oo, t + tt)
                acc_ref[hs, cs] = acc_in[hs, cs] + o * mask[:, cs]
                sum_ref[ss, cs] = sum_in[ss, cs] + t * mask[:, cs]


def careful(own_ref, full_refs, far_ref, qt_ref, out_ref, s_ref):
    refs = (own_ref, *full_refs, far_ref)
    lanes = 128
    key0 = lax.broadcasted_iota(jnp.int32, (HALF, lanes), 0)
    row0 = lax.broadcasted_iota(jnp.int32, (HALF, lanes), 1)
    mask = row_mask(own_ref)

    def one(step, carry):
        h, c = step // 4, step % 4
        hs = pl.ds(pl.multiple_of(h * DEPTH, DEPTH), DEPTH)
        cs = pl.ds(pl.multiple_of(c * lanes, lanes), lanes)
        qt = qt_ref[hs, cs]
        row = row0 + c * lanes
        both = [docs(own_ref, r // 2)[:, r % 2 * 128 : r % 2 * 128 + 128] for r in range(4)]
        own_row = mrow = None
        for r in range(4):
            picked = jnp.where(c == r, both[r], 0.0)
            m = jnp.where(c == r, mask[:, r * 128 : (r + 1) * 128], 0.0)
            own_row = picked if own_row is None else own_row + picked
            mrow = m if mrow is None else mrow + m
        for n, ref in enumerate(refs):
            for k in range(2):
                key = key0 + k * HALF
                col = column(docs(ref, k))
                if n == 0:
                    keep = (col == own_row) & (key <= row)
                else:
                    keep = (column(key_match(own_ref, ref, k)) * mrow) > 0.5
                    if ref is far_ref:
                        keep = keep & (key > row)
                s = dot(keys(ref, k), qt) * SCALE
                at = (2 * n + k) * HALF
                s_ref[at : at + HALF, :] = jnp.where(keep, s, NEG)
        top = jnp.max(s_ref[...], axis=0, keepdims=True)
        o, t = jnp.zeros((DEPTH, lanes), F32), jnp.zeros((1, lanes), F32)
        for n, ref in enumerate(refs):
            for k in range(2):
                at = (2 * n + k) * HALF
                e = jnp.exp2(s_ref[at : at + HALF, :] - top)
                t = t + jnp.sum(e, axis=0, keepdims=True)
                o = o + dot(values(ref, k), e.astype(BF16))
        out_ref[cs, hs] = (o / t).T.astype(BF16)
        return carry

    lax.fori_loop(0, HEADS * 4, one, 0)


def last_block(
    own_ref, e0_ref, pa_ref, e1_ref, pb_ref, e2_ref, qt_ref, acc_in, sum_in,
    out_ref, s_ref, good_ref,
):
    def put(h, acc, sums):
        t = jnp.sum(sums, axis=0, keepdims=True)
        good_ref[h : h + 1, :] = jnp.where((t > LOW) & (t < HIGH), 1.0, 0.0)
        out_ref[:, h * DEPTH : (h + 1) * DEPTH] = (acc * (1.0 / t)).T.astype(BF16)

    seen = any_seen(own_ref, e2_ref)

    @pl.when(seen)
    def _():
        full_heads(own_ref, e2_ref, qt_ref, acc_in, sum_in, put)

    @pl.when(jnp.logical_not(seen))
    def _():
        for h in range(HEADS):
            hs = slice(h * DEPTH, (h + 1) * DEPTH)
            put(h, acc_in[hs, :], sum_in[h * 8 : (h + 1) * 8, :])

    @pl.when(jnp.min(good_ref[...]) < 0.5)
    def _():
        careful(own_ref, (e0_ref, pa_ref, e1_ref, e2_ref), pb_ref, qt_ref, out_ref, s_ref)


def local(queries, k, v, doc_ids):
    size = lax.axis_size("ctx")
    block = jax.ShapeDtypeStruct(BLOCK, BF16)
    qt_out = jax.ShapeDtypeStruct(QT, BF16)
    acc_out = jax.ShapeDtypeStruct(QT, F32)
    sum_out = jax.ShapeDtypeStruct(SUMS, F32)
    work = 4 * ROWS * ROWS * DEPTH * HEADS
    exps = ROWS * ROWS * HEADS

    def move(x, pairs):
        return lax.ppermute(x, "ctx", [(a, b) for a, b in pairs if 0 <= b < size])

    own = call(pack, block)(k, v, doc_ids.reshape(2, HALF))
    pa = move(own, [(i, i + (1 if i % 2 else 3)) for i in range(size)])
    pb = move(own, [(i, i + 4) for i in range(size)])
    e0 = move(own, [(i, i + 1) for i in range(0, size, 2)])
    e1 = move(pa, [(i, i ^ 1) for i in range(size)])
    e2 = move(pb, [(i, i - 1) for i in range(1, size, 2)])

    qt, acc, sums = call(
        own_block, (qt_out, acc_out, sum_out), None, work * 2, exps
    )(queries, own, e0)
    full = call(full_block, (acc_out, sum_out), {3: 0, 4: 1}, work * 2, exps)
    far = call(far_block, (acc_out, sum_out), {3: 0, 4: 1}, work * 3 // 2, exps)
    acc, sums = full(own, pa, qt, acc, sums)
    acc, sums = full(own, e1, qt, acc, sums)
    acc, sums = far(own, pb, qt, acc, sums)
    return call(
        last_block,
        jax.ShapeDtypeStruct(queries.shape, BF16),
        scratch=(pltpu.VMEM((12 * HALF, 128), F32), pltpu.VMEM((HEADS, ROWS), F32)),
    )(own, e0, pa, e1, pb, e2, qt, acc, sums)


def solution(mesh):
    return jax.shard_map(
        local,
        mesh=mesh,
        in_specs=(P("ctx", None), P("ctx", None), P("ctx", None), P("ctx")),
        out_specs=P("ctx", None),
        check_vma=False,
    )
```

```python
import jax
import jax.numpy as jnp
from jax import lax
from jax.experimental import pallas as pl
from jax.experimental.pallas import tpu as pltpu
from jax.sharding import PartitionSpec as P

ROWS = 512
HALF = 256
DEPTH = 128
HEADS = 8
SCALE = 1.4426950408889634 / DEPTH**0.5
NEG = -1e30
LOW, HIGH = 2.0**-60, 2.0**100
VM = pl.BlockSpec(memory_space=pltpu.VMEM)
BLOCK = (ROWS + 16, HALF)
QT = (HEADS * DEPTH, ROWS)
SUMS = (HEADS * 8, ROWS)
F32 = jnp.float32
BF16 = jnp.bfloat16


ANY = pl.BlockSpec(memory_space=pl.ANY)
BIAS = pltpu.VMEM((ROWS + HALF, HALF), F32)


def call(body, out, ins=None, outs=None, scratch=()):
    return pl.pallas_call(
        body,
        out_shape=out,
        **({} if ins is None else {"in_specs": ins}),
        out_specs=outs or jax.tree.map(lambda _: VM, out),
        scratch_shapes=scratch,
        cost_estimate=pl.CostEstimate(flops=1, bytes_accessed=1, transcendentals=0),
        compiler_params=pltpu.CompilerParams(vmem_limit_bytes=16 << 20),
    )


def in_hbm(x):
    return pltpu.with_memory_space_constraint(x, pltpu.HBM)


def pack(k_ref, v_ref, d_ref, q_ref, o_ref, q_s, v_s, d_s, sem):
    copies = [
        pltpu.make_async_copy(d_ref, d_s.at[0], sem.at[0]),
        pltpu.make_async_copy(v_ref, v_s, sem.at[1]),
        pltpu.make_async_copy(k_ref.at[0:HALF, :], o_ref.at[0:HALF, 0:DEPTH], sem.at[2]),
        pltpu.make_async_copy(
            k_ref.at[HALF:ROWS, :], o_ref.at[0:HALF, DEPTH:HALF], sem.at[3]
        ),
        pltpu.make_async_copy(q_ref, q_s, sem.at[4]),
    ]
    for c in copies:
        c.start()
    copies[0].wait()
    d = (d_s[...] + 1).astype(F32)
    o_ref[ROWS : ROWS + 16, :] = jnp.concatenate(
        [d[:, 0:HALF], d[:, HALF:ROWS], jnp.zeros((14, HALF), F32)], axis=0
    ).astype(BF16)
    copies[1].wait()
    vt = v_s[...].T
    o_ref[HALF : HALF + DEPTH, :] = vt[:, 0:HALF]
    o_ref[HALF + DEPTH : ROWS, :] = vt[:, HALF:ROWS]
    for c in copies[2:]:
        c.wait()


def tie(x_ref, after_ref, o_ref):
    o_ref[...] = x_ref[...]


def join(own_ref, pa_ref, after_ref, o_ref):
    o_ref[0 : BLOCK[0], :] = own_ref[...]
    o_ref[BLOCK[0] :, :] = pa_ref[...]


def gathered(g_ref, at):
    start = pl.multiple_of(at * BLOCK[0], 16)
    return g_ref.at[pl.ds(start, BLOCK[0]), :]


def near_parts(g_ref):
    core = lax.axis_index("ctx") % 2
    return gathered(g_ref, 1 - core), gathered(g_ref, 3 - 2 * core)


def keys(ref, half):
    return ref[0:HALF, half * DEPTH : (half + 1) * DEPTH]


def values(ref, half):
    return ref[HALF + half * DEPTH : HALF + (half + 1) * DEPTH, :]


def docs(ref, half):
    return ref[ROWS : ROWS + 16, :].astype(F32)[half : half + 1, :]


def column(row):
    return jnp.broadcast_to(row, (DEPTH, row.shape[1])).T


def widen(col, lanes):
    return jnp.concatenate([col] * (lanes // DEPTH), axis=1)


def first_doc(own_ref):
    return docs(own_ref, 0)[:, 0:1]


def row_mask(own_ref):
    both = jnp.concatenate([docs(own_ref, 0), docs(own_ref, 1)], axis=1)
    return jnp.where(both == first_doc(own_ref), 1.0, 0.0)


def key_match(own_ref, ref, half):
    return jnp.where(docs(ref, half) == first_doc(own_ref), 1.0, 0.0)


def key_bias(own_ref, ref, half):
    return column((1.0 - key_match(own_ref, ref, half)) * NEG)


def dot(a, b):
    return jnp.dot(a, b, preferred_element_type=F32)


def fold(e):
    return jnp.sum(e.reshape(e.shape[0] // 8, 8, e.shape[1]), axis=0)


def all_keys(ref):
    return jnp.concatenate([keys(ref, 0), keys(ref, 1)], axis=0)


def all_values(ref):
    return jnp.concatenate([values(ref, 0), values(ref, 1)], axis=1)


def head(h):
    return slice(h * DEPTH, (h + 1) * DEPTH)


def eight(h):
    return slice(h * 8, (h + 1) * 8)


def staged(units, first, rest, depth=1):
    held = [first(u) for u in units[:depth]]
    for i, u in enumerate(units):
        if i + depth < len(units):
            held.append(first(units[i + depth]))
        rest(u, held.pop(0))


def triangle(strict):
    key = lax.broadcasted_iota(jnp.int32, (HALF, HALF), 0)
    row = lax.broadcasted_iota(jnp.int32, (HALF, HALF), 1)
    keep = key > row if strict else key <= row
    return jnp.where(keep, 0.0, NEG)


def any_seen(own_ref, ref):
    seen = key_match(own_ref, ref, 0) + key_match(own_ref, ref, 1)
    return jnp.max(seen) > 0.5


def keeper(acc_ref, sum_ref):
    def put(h, acc, sums):
        acc_ref[head(h), :] = acc
        sum_ref[eight(h), :] = sums

    return put


def full_heads(own_ref, refs, qt_ref, acc_in, sum_in, put):
    mask = row_mask(own_ref)
    cat = lambda parts, axis: jnp.concatenate(parts, axis=axis)
    col = cat([key_bias(own_ref, x, k) for x in refs for k in range(2)], 0)
    kk = cat([cat([all_keys(x) for x in refs], 0), col.astype(BF16)], 1)
    vv = cat([all_values(x) for x in refs], 1)
    at = lax.broadcasted_iota(jnp.int32, (DEPTH, ROWS), 0)
    one = jnp.where(at == 0, 1.0, 0.0).astype(BF16)

    def first(h):
        return dot(kk, cat([qt_ref[head(h), :], one], 0))

    def rest(h, s):
        e = jnp.exp2(s * SCALE)
        o = dot(vv, e.astype(BF16))
        put(h, acc_in[head(h), :] + o * mask, sum_in[eight(h), :] + fold(e) * mask)

    staged(range(HEADS), first, rest)


def cut_heads(qt_ref, b_ref, kk, vv, cut, put):
    def first(u):
        h, r = u
        return dot(kk[r], qt_ref[head(h), r * HALF : (r + 1) * HALF])

    def rest(u, s):
        h, r = u
        e = jnp.exp2(s * SCALE + b_ref[cut[r], :])
        put(h, slice(r * HALF, (r + 1) * HALF), dot(vv[r], e.astype(BF16)), fold(e))

    staged([(h, r) for h in range(HEADS) for r in range(2)], first, rest, 2)


def own_block(q_ref, own_ref, qt_ref, acc_ref, sum_ref, b_ref):
    for h in range(HEADS):
        qt_ref[head(h), :] = q_ref[:, head(h)].T
    rows = [docs(own_ref, 0), docs(own_ref, 1)]
    cols = [widen(column(r), HALF) for r in rows]
    apart = lambda k, r: jnp.where(cols[k] == rows[r], 0.0, NEG)
    tri = triangle(False)
    b_ref[0:HALF, :] = apart(0, 1)
    b_ref[HALF:ROWS, :] = apart(1, 1) + tri
    b_ref[ROWS : ROWS + HALF, :] = apart(0, 0) + tri

    def put(h, cs, o, t):
        acc_ref[head(h), cs] = o
        sum_ref[eight(h), cs] = t

    cut_heads(
        qt_ref,
        b_ref,
        (keys(own_ref, 0), all_keys(own_ref)),
        (values(own_ref, 0), all_values(own_ref)),
        (slice(ROWS, ROWS + HALF), slice(0, ROWS)),
        put,
    )


def near_blocks(own_ref, g_ref, qt_ref, acc_in, sum_in, acc_ref, sum_ref):
    parts = near_parts(g_ref)
    seen = any_seen(own_ref, parts[0]) | any_seen(own_ref, parts[1])

    @pl.when(seen)
    def _():
        full_heads(own_ref, parts, qt_ref, acc_in, sum_in, keeper(acc_ref, sum_ref))

    @pl.when(jnp.logical_not(seen))
    def _():
        acc_ref[...] = acc_in[...]
        sum_ref[...] = sum_in[...]


def far_block(own_ref, ref, qt_ref, acc_in, sum_in, acc_ref, sum_ref, b_ref):
    seen = any_seen(own_ref, ref)

    @pl.when(seen)
    def _():
        mask = row_mask(own_ref)
        cols = [widen(key_bias(own_ref, ref, k), HALF) for k in range(2)]
        tri = triangle(True)
        b_ref[0:HALF, :] = cols[0] + tri
        b_ref[HALF:ROWS, :] = cols[1]
        b_ref[ROWS : ROWS + HALF, :] = cols[1] + tri

        def put(h, cs, o, t):
            acc_ref[head(h), cs] = acc_in[head(h), cs] + o * mask[:, cs]
            sum_ref[eight(h), cs] = sum_in[eight(h), cs] + t * mask[:, cs]

        cut_heads(
            qt_ref,
            b_ref,
            (all_keys(ref), keys(ref, 1)),
            (all_values(ref), values(ref, 1)),
            (slice(0, ROWS), slice(ROWS, ROWS + HALF)),
            put,
        )

    @pl.when(jnp.logical_not(seen))
    def _():
        acc_ref[...] = acc_in[...]
        sum_ref[...] = sum_in[...]


def careful(own_ref, full_refs, far_ref, qt_ref, out_ref, s_ref):
    refs = (own_ref, *full_refs, far_ref)
    lanes = 128
    key0 = lax.broadcasted_iota(jnp.int32, (HALF, lanes), 0)
    row0 = lax.broadcasted_iota(jnp.int32, (HALF, lanes), 1)
    mask = row_mask(own_ref)

    def one(step, carry):
        h, c = step // 4, step % 4
        hs = pl.ds(pl.multiple_of(h * DEPTH, DEPTH), DEPTH)
        cs = pl.ds(pl.multiple_of(c * lanes, lanes), lanes)
        qt = qt_ref[hs, cs]
        row = row0 + c * lanes
        both = [docs(own_ref, r // 2)[:, r % 2 * 128 : r % 2 * 128 + 128] for r in range(4)]
        own_row = mrow = None
        for r in range(4):
            picked = jnp.where(c == r, both[r], 0.0)
            m = jnp.where(c == r, mask[:, r * 128 : (r + 1) * 128], 0.0)
            own_row = picked if own_row is None else own_row + picked
            mrow = m if mrow is None else mrow + m
        for n, ref in enumerate(refs):
            for k in range(2):
                key = key0 + k * HALF
                col = column(docs(ref, k))
                if n == 0:
                    keep = (col == own_row) & (key <= row)
                else:
                    keep = (column(key_match(own_ref, ref, k)) * mrow) > 0.5
                    if ref is far_ref:
                        keep = keep & (key > row)
                s = dot(keys(ref, k), qt) * SCALE
                at = (2 * n + k) * HALF
                s_ref[at : at + HALF, :] = jnp.where(keep, s, NEG)
        top = jnp.max(s_ref[...], axis=0, keepdims=True)
        o, t = jnp.zeros((DEPTH, lanes), F32), jnp.zeros((1, lanes), F32)
        for n, ref in enumerate(refs):
            for k in range(2):
                at = (2 * n + k) * HALF
                e = jnp.exp2(s_ref[at : at + HALF, :] - top)
                t = t + jnp.sum(e, axis=0, keepdims=True)
                o = o + dot(values(ref, k), e.astype(BF16))
        out_ref[cs, hs] = (o / t).T.astype(BF16)
        return carry

    lax.fori_loop(0, HEADS * 4, one, 0)


def last_block(
    own_ref, g_ref, pb_ref, e2_ref, qt_ref, acc_in, sum_in,
    out_ref, x_s, o_s, s_ref, good_ref, sem,
):
    core = lax.axis_index("ctx") % 2

    @pl.when(core == 0)
    def _():
        x_s[...] = e2_ref[...]

    @pl.when(core == 1)
    def _():
        x_s[...] = g_ref[3 * BLOCK[0] :, :]

    copies = [
        pltpu.make_async_copy(o_s.at[:, head(h)], out_ref.at[:, head(h)], sem.at[h])
        for h in range(HEADS)
    ]

    def put(h, acc, sums):
        t = jnp.sum(sums, axis=0, keepdims=True)
        good_ref[h : h + 1, :] = jnp.where((t > LOW) & (t < HIGH), 1.0, 0.0)
        o_s[:, head(h)] = (acc * (1.0 / t)).astype(BF16).T
        copies[h].start()

    seen = any_seen(own_ref, x_s)

    @pl.when(seen)
    def _():
        full_heads(own_ref, (x_s,), qt_ref, acc_in, sum_in, put)

    @pl.when(jnp.logical_not(seen))
    def _():
        for h in range(HEADS):
            put(h, acc_in[head(h), :], sum_in[eight(h), :])

    for c in copies:
        c.wait()

    @pl.when(jnp.min(good_ref[...]) < 0.5)
    def _():
        careful(own_ref, (*near_parts(g_ref), x_s), pb_ref, qt_ref, o_s, s_ref)
        for c in copies:
            c.start()
        for c in copies:
            c.wait()


def local(queries, k, v, doc_ids):
    size = lax.axis_size("ctx")
    block = jax.ShapeDtypeStruct(BLOCK, BF16)
    qt_out = jax.ShapeDtypeStruct(QT, BF16)
    acc_out = jax.ShapeDtypeStruct(QT, F32)
    sum_out = jax.ShapeDtypeStruct(SUMS, F32)
    dma = pltpu.SemaphoreType.DMA

    def move(x, pairs):
        return lax.ppermute(x, "ctx", [(a, b) for a, b in pairs if 0 <= b < size])

    own, q = call(
        pack,
        (block, jax.ShapeDtypeStruct(queries.shape, BF16)),
        (ANY, ANY, ANY, ANY),
        scratch=(
            pltpu.VMEM((ROWS, DEPTH), BF16),
            pltpu.VMEM((1, ROWS), jnp.int32),
            dma((5,)),
        ),
    )(in_hbm(k), in_hbm(v), in_hbm(doc_ids), in_hbm(queries))
    pa = move(own, [(i, i + (1 if i % 2 else 3)) for i in range(size)])
    pb = move(own, [(i, i + 4) for i in range(size)])
    qt, acc, sums = call(own_block, (qt_out, acc_out, sum_out), scratch=(BIAS,))(q, own)

    pair = jax.ShapeDtypeStruct((2 * BLOCK[0], HALF), BF16)
    both = call(join, pair, (VM, VM, ANY))(own, pa, sums)
    cores = [[i, i + 1] for i in range(0, size, 2)]
    g = lax.all_gather(both, "ctx", axis_index_groups=cores, tiled=True)
    acc, sums = call(near_blocks, (acc_out, sum_out))(own, g, qt, acc, sums)
    pb = call(tie, block, (VM, ANY))(pb, sums)
    e2 = move(pb, [(i, i - 1) for i in range(1, size, 2)])
    acc, sums = call(far_block, (acc_out, sum_out), scratch=(BIAS,))(
        own, pb, qt, acc, sums
    )
    return call(
        last_block,
        jax.ShapeDtypeStruct(queries.shape, BF16),
        outs=ANY,
        scratch=(
            pltpu.VMEM(BLOCK, BF16),
            pltpu.VMEM((ROWS, HEADS * DEPTH), BF16),
            pltpu.VMEM((10 * HALF, 128), F32),
            pltpu.VMEM((HEADS, ROWS), F32),
            dma((HEADS,)),
        ),
    )(own, g, pb, e2, qt, acc, sums)


def solution(mesh):
    return jax.shard_map(
        local,
        mesh=mesh,
        in_specs=(P("ctx", None), P("ctx", None), P("ctx", None), P("ctx")),
        out_specs=P("ctx", None),
        check_vma=False,
    )
```

```python
import jax
import jax.numpy as jnp
from jax import lax
from jax.experimental import pallas as pl
from jax.experimental.pallas import tpu as pltpu
from jax.sharding import PartitionSpec as P

ROWS = 512
HALF = 256
DEPTH = 128
HEADS = 8
SCALE = 1.4426950408889634 / DEPTH**0.5
NEG = -1e30
LOW, HIGH = 2.0**-60, 2.0**100
VM = pl.BlockSpec(memory_space=pltpu.VMEM)
BLOCK = (ROWS + 16, HALF)
QT = (HEADS * DEPTH, ROWS)
SUMS = (HEADS * 8, ROWS)
F32 = jnp.float32
BF16 = jnp.bfloat16


ANY = pl.BlockSpec(memory_space=pl.ANY)
BIAS = pltpu.VMEM((ROWS + HALF, HALF), F32)


def call(body, out, ins=None, outs=None, scratch=()):
    return pl.pallas_call(
        body,
        out_shape=out,
        **({} if ins is None else {"in_specs": ins}),
        out_specs=outs or jax.tree.map(lambda _: VM, out),
        scratch_shapes=scratch,
        cost_estimate=pl.CostEstimate(flops=1, bytes_accessed=1, transcendentals=0),
        compiler_params=pltpu.CompilerParams(vmem_limit_bytes=16 << 20),
    )


def in_hbm(x):
    return pltpu.with_memory_space_constraint(x, pltpu.HBM)


def pack(k_ref, v_ref, d_ref, q_ref, o_ref, q_s, v_s, d_s, sem):
    copies = [
        pltpu.make_async_copy(d_ref, d_s.at[0], sem.at[0]),
        pltpu.make_async_copy(v_ref, v_s, sem.at[1]),
        pltpu.make_async_copy(k_ref.at[0:HALF, :], o_ref.at[0:HALF, 0:DEPTH], sem.at[2]),
        pltpu.make_async_copy(
            k_ref.at[HALF:ROWS, :], o_ref.at[0:HALF, DEPTH:HALF], sem.at[3]
        ),
        pltpu.make_async_copy(q_ref, q_s, sem.at[4]),
    ]
    for c in copies:
        c.start()
    copies[0].wait()
    d = (d_s[...] + 1).astype(F32)
    o_ref[ROWS : ROWS + 16, :] = jnp.concatenate(
        [d[:, 0:HALF], d[:, HALF:ROWS], jnp.zeros((14, HALF), F32)], axis=0
    ).astype(BF16)
    copies[1].wait()
    vt = v_s[...].T
    o_ref[HALF : HALF + DEPTH, :] = vt[:, 0:HALF]
    o_ref[HALF + DEPTH : ROWS, :] = vt[:, HALF:ROWS]
    for c in copies[2:]:
        c.wait()


def join(own_ref, pa_ref, pb_ref, after_ref, o_ref):
    core = lax.axis_index("ctx") % 2
    first, second = slice(0, BLOCK[0]), slice(BLOCK[0], 2 * BLOCK[0])

    @pl.when(core == 0)
    def _():
        o_ref[first, :] = own_ref[...]
        o_ref[second, :] = pa_ref[...]

    @pl.when(core == 1)
    def _():
        o_ref[first, :] = pa_ref[...]
        o_ref[second, :] = pb_ref[...]


def halves(ex_ref):
    return ex_ref.at[0 : BLOCK[0], :], ex_ref.at[BLOCK[0] : 2 * BLOCK[0], :]


def keys(ref, half):
    return ref[0:HALF, half * DEPTH : (half + 1) * DEPTH]


def values(ref, half):
    return ref[HALF + half * DEPTH : HALF + (half + 1) * DEPTH, :]


def docs(ref, half):
    return ref[ROWS : ROWS + 16, :].astype(F32)[half : half + 1, :]


def column(row):
    return jnp.broadcast_to(row, (DEPTH, row.shape[1])).T


def widen(col, lanes):
    return jnp.concatenate([col] * (lanes // DEPTH), axis=1)


def first_doc(own_ref):
    return docs(own_ref, 0)[:, 0:1]


def row_mask(own_ref):
    both = jnp.concatenate([docs(own_ref, 0), docs(own_ref, 1)], axis=1)
    return jnp.where(both == first_doc(own_ref), 1.0, 0.0)


def key_match(own_ref, ref, half):
    return jnp.where(docs(ref, half) == first_doc(own_ref), 1.0, 0.0)


def key_bias(own_ref, ref, half):
    return column((1.0 - key_match(own_ref, ref, half)) * NEG)


def dot(a, b):
    return jnp.dot(a, b, preferred_element_type=F32)


def fold(e):
    return jnp.sum(e.reshape(e.shape[0] // 8, 8, e.shape[1]), axis=0)


def all_keys(ref):
    return jnp.concatenate([keys(ref, 0), keys(ref, 1)], axis=0)


def all_values(ref):
    return jnp.concatenate([values(ref, 0), values(ref, 1)], axis=1)


def head(h):
    return slice(h * DEPTH, (h + 1) * DEPTH)


def eight(h):
    return slice(h * 8, (h + 1) * 8)


def staged(units, first, rest, depth=1):
    held = [first(u) for u in units[:depth]]
    for i, u in enumerate(units):
        if i + depth < len(units):
            held.append(first(units[i + depth]))
        rest(u, held.pop(0))


def triangle(strict):
    key = lax.broadcasted_iota(jnp.int32, (HALF, HALF), 0)
    row = lax.broadcasted_iota(jnp.int32, (HALF, HALF), 1)
    keep = key > row if strict else key <= row
    return jnp.where(keep, 0.0, NEG)


def any_seen(own_ref, ref):
    seen = key_match(own_ref, ref, 0) + key_match(own_ref, ref, 1)
    return jnp.max(seen) > 0.5


def keeper(acc_ref, sum_ref):
    def put(h, acc, sums):
        acc_ref[head(h), :] = acc
        sum_ref[eight(h), :] = sums

    return put


def full_heads(own_ref, refs, qt_ref, acc_in, sum_in, put):
    mask = row_mask(own_ref)
    cat = lambda parts, axis: jnp.concatenate(parts, axis=axis)
    col = cat([key_bias(own_ref, x, k) for x in refs for k in range(2)], 0)
    kk = cat([cat([all_keys(x) for x in refs], 0), col.astype(BF16)], 1)
    vv = cat([all_values(x) for x in refs], 1)
    at = lax.broadcasted_iota(jnp.int32, (DEPTH, ROWS), 0)
    one = jnp.where(at == 0, 1.0, 0.0).astype(BF16)

    def first(h):
        return dot(kk, cat([qt_ref[head(h), :], one], 0))

    def rest(h, s):
        e = jnp.exp2(s * SCALE)
        o = dot(vv, e.astype(BF16))
        put(h, acc_in[head(h), :] + o * mask, sum_in[eight(h), :] + fold(e) * mask)

    staged(range(HEADS), first, rest)


def cut_heads(qt_ref, b_ref, kk, vv, cut, put):
    def first(u):
        h, r = u
        return dot(kk[r], qt_ref[head(h), r * HALF : (r + 1) * HALF])

    def rest(u, s):
        h, r = u
        e = jnp.exp2(s * SCALE + b_ref[cut[r], :])
        put(h, slice(r * HALF, (r + 1) * HALF), dot(vv[r], e.astype(BF16)), fold(e))

    staged([(h, r) for h in range(HEADS) for r in range(2)], first, rest, 2)


def own_block(q_ref, own_ref, qt_ref, acc_ref, sum_ref, b_ref):
    for h in range(HEADS):
        qt_ref[head(h), :] = q_ref[:, head(h)].T
    rows = [docs(own_ref, 0), docs(own_ref, 1)]
    cols = [widen(column(r), HALF) for r in rows]
    apart = lambda k, r: jnp.where(cols[k] == rows[r], 0.0, NEG)
    tri = triangle(False)
    b_ref[0:HALF, :] = apart(0, 1)
    b_ref[HALF:ROWS, :] = apart(1, 1) + tri
    b_ref[ROWS : ROWS + HALF, :] = apart(0, 0) + tri

    def put(h, cs, o, t):
        acc_ref[head(h), cs] = o
        sum_ref[eight(h), cs] = t

    cut_heads(
        qt_ref,
        b_ref,
        (keys(own_ref, 0), all_keys(own_ref)),
        (values(own_ref, 0), all_values(own_ref)),
        (slice(ROWS, ROWS + HALF), slice(0, ROWS)),
        put,
    )


def full_block(own_ref, ref, qt_ref, acc_in, sum_in, acc_ref, sum_ref):
    seen = any_seen(own_ref, ref)

    @pl.when(seen)
    def _():
        full_heads(own_ref, (ref,), qt_ref, acc_in, sum_in, keeper(acc_ref, sum_ref))

    @pl.when(jnp.logical_not(seen))
    def _():
        acc_ref[...] = acc_in[...]
        sum_ref[...] = sum_in[...]


def far_block(own_ref, ref, qt_ref, acc_in, sum_in, acc_ref, sum_ref, b_ref):
    seen = any_seen(own_ref, ref)

    @pl.when(seen)
    def _():
        mask = row_mask(own_ref)
        cols = [widen(key_bias(own_ref, ref, k), HALF) for k in range(2)]
        tri = triangle(True)
        b_ref[0:HALF, :] = cols[0] + tri
        b_ref[HALF:ROWS, :] = cols[1]
        b_ref[ROWS : ROWS + HALF, :] = cols[1] + tri

        def put(h, cs, o, t):
            acc_ref[head(h), cs] = acc_in[head(h), cs] + o * mask[:, cs]
            sum_ref[eight(h), cs] = sum_in[eight(h), cs] + t * mask[:, cs]

        cut_heads(
            qt_ref,
            b_ref,
            (all_keys(ref), keys(ref, 1)),
            (all_values(ref), values(ref, 1)),
            (slice(0, ROWS), slice(ROWS, ROWS + HALF)),
            put,
        )

    @pl.when(jnp.logical_not(seen))
    def _():
        acc_ref[...] = acc_in[...]
        sum_ref[...] = sum_in[...]


def careful(own_ref, full_refs, far_ref, qt_ref, out_ref, s_ref):
    refs = (own_ref, *full_refs, far_ref)
    lanes = 128
    key0 = lax.broadcasted_iota(jnp.int32, (HALF, lanes), 0)
    row0 = lax.broadcasted_iota(jnp.int32, (HALF, lanes), 1)
    mask = row_mask(own_ref)

    def one(step, carry):
        h, c = step // 4, step % 4
        hs = pl.ds(pl.multiple_of(h * DEPTH, DEPTH), DEPTH)
        cs = pl.ds(pl.multiple_of(c * lanes, lanes), lanes)
        qt = qt_ref[hs, cs]
        row = row0 + c * lanes
        both = [docs(own_ref, r // 2)[:, r % 2 * 128 : r % 2 * 128 + 128] for r in range(4)]
        own_row = mrow = None
        for r in range(4):
            picked = jnp.where(c == r, both[r], 0.0)
            m = jnp.where(c == r, mask[:, r * 128 : (r + 1) * 128], 0.0)
            own_row = picked if own_row is None else own_row + picked
            mrow = m if mrow is None else mrow + m
        for n, ref in enumerate(refs):
            for k in range(2):
                key = key0 + k * HALF
                col = column(docs(ref, k))
                if n == 0:
                    keep = (col == own_row) & (key <= row)
                else:
                    keep = (column(key_match(own_ref, ref, k)) * mrow) > 0.5
                    if ref is far_ref:
                        keep = keep & (key > row)
                s = dot(keys(ref, k), qt) * SCALE
                at = (2 * n + k) * HALF
                s_ref[at : at + HALF, :] = jnp.where(keep, s, NEG)
        top = jnp.max(s_ref[...], axis=0, keepdims=True)
        o, t = jnp.zeros((DEPTH, lanes), F32), jnp.zeros((1, lanes), F32)
        for n, ref in enumerate(refs):
            for k in range(2):
                at = (2 * n + k) * HALF
                e = jnp.exp2(s_ref[at : at + HALF, :] - top)
                t = t + jnp.sum(e, axis=0, keepdims=True)
                o = o + dot(values(ref, k), e.astype(BF16))
        out_ref[cs, hs] = (o / t).T.astype(BF16)
        return carry

    lax.fori_loop(0, HEADS * 4, one, 0)


def last_block(
    own_ref, pa_ref, pb_ref, ex_ref, qt_ref, acc_in, sum_in,
    out_ref, o_s, s_ref, good_ref, sem,
):
    parts = halves(ex_ref)
    copies = [
        pltpu.make_async_copy(o_s.at[:, head(h)], out_ref.at[:, head(h)], sem.at[h])
        for h in range(HEADS)
    ]

    def put(h, acc, sums):
        t = jnp.sum(sums, axis=0, keepdims=True)
        good_ref[h : h + 1, :] = jnp.where((t > LOW) & (t < HIGH), 1.0, 0.0)
        o_s[:, head(h)] = (acc * (1.0 / t)).astype(BF16).T
        copies[h].start()

    seen = any_seen(own_ref, parts[0]) | any_seen(own_ref, parts[1])

    @pl.when(seen)
    def _():
        full_heads(own_ref, parts, qt_ref, acc_in, sum_in, put)

    @pl.when(jnp.logical_not(seen))
    def _():
        for h in range(HEADS):
            put(h, acc_in[head(h), :], sum_in[eight(h), :])

    for c in copies:
        c.wait()

    @pl.when(jnp.min(good_ref[...]) < 0.5)
    def _():
        careful(own_ref, (pa_ref, *parts), pb_ref, qt_ref, o_s, s_ref)
        for c in copies:
            c.start()
        for c in copies:
            c.wait()


def local(queries, k, v, doc_ids):
    size = lax.axis_size("ctx")
    block = jax.ShapeDtypeStruct(BLOCK, BF16)
    qt_out = jax.ShapeDtypeStruct(QT, BF16)
    acc_out = jax.ShapeDtypeStruct(QT, F32)
    sum_out = jax.ShapeDtypeStruct(SUMS, F32)
    dma = pltpu.SemaphoreType.DMA

    def move(x, pairs):
        return lax.ppermute(x, "ctx", [(a, b) for a, b in pairs if 0 <= b < size])

    own, q = call(
        pack,
        (block, jax.ShapeDtypeStruct(queries.shape, BF16)),
        (ANY, ANY, ANY, ANY),
        scratch=(
            pltpu.VMEM((ROWS, DEPTH), BF16),
            pltpu.VMEM((1, ROWS), jnp.int32),
            dma((5,)),
        ),
    )(in_hbm(k), in_hbm(v), in_hbm(doc_ids), in_hbm(queries))
    pa = move(own, [(i, i + (1 if i % 2 else 3)) for i in range(size)])
    pb = move(own, [(i, i + 4) for i in range(size)])
    qt, acc, sums = call(own_block, (qt_out, acc_out, sum_out), scratch=(BIAS,))(q, own)

    acc, sums = call(full_block, (acc_out, sum_out))(own, pa, qt, acc, sums)

    pair = jax.ShapeDtypeStruct((2 * BLOCK[0], HALF), BF16)
    ex = call(join, pair, (VM, VM, VM, ANY))(own, pa, pb, sums)
    ex = move(ex, [(i, i ^ 1) for i in range(size)])
    acc, sums = call(far_block, (acc_out, sum_out), scratch=(BIAS,))(
        own, pb, qt, acc, sums
    )
    return call(
        last_block,
        jax.ShapeDtypeStruct(queries.shape, BF16),
        outs=ANY,
        scratch=(
            pltpu.VMEM((ROWS, HEADS * DEPTH), BF16),
            pltpu.VMEM((10 * HALF, 128), F32),
            pltpu.VMEM((HEADS, ROWS), F32),
            dma((HEADS,)),
        ),
    )(own, pa, pb, ex, qt, acc, sums)


def solution(mesh):
    return jax.shard_map(
        local,
        mesh=mesh,
        in_specs=(P("ctx", None), P("ctx", None), P("ctx", None), P("ctx")),
        out_specs=P("ctx", None),
        check_vma=False,
    )
```

```python
import jax
import jax.numpy as jnp
from jax import lax
from jax.experimental import pallas as pl
from jax.experimental.pallas import tpu as pltpu
from jax.sharding import PartitionSpec as P

ROWS = 512
HALF = 256
DEPTH = 128
HEADS = 8
SCALE = 1.4426950408889634 / DEPTH**0.5
NEG = -1e30
LOW, HIGH = 2.0**-60, 2.0**100
VM = pl.BlockSpec(memory_space=pltpu.VMEM)
SENT = (ROWS + 32, HALF)
BLOCK = (ROWS + 16, HALF)
QT = (HEADS * DEPTH, ROWS)
SUMS = (HEADS * 8, ROWS)
F32 = jnp.float32
BF16 = jnp.bfloat16


ANY = pl.BlockSpec(memory_space=pl.ANY)
BIAS = pltpu.VMEM((ROWS + HALF, HALF), F32)
TRI = pltpu.VMEM((HALF, HALF), F32)


def call(body, out, ins=None, outs=None, scratch=()):
    return pl.pallas_call(
        body,
        out_shape=out,
        **({} if ins is None else {"in_specs": ins}),
        out_specs=outs or jax.tree.map(lambda _: VM, out),
        scratch_shapes=scratch,
        cost_estimate=pl.CostEstimate(flops=1, bytes_accessed=1, transcendentals=0),
        compiler_params=pltpu.CompilerParams(vmem_limit_bytes=16 << 20),
    )


def in_hbm(x):
    return pltpu.with_memory_space_constraint(x, pltpu.HBM)


def pack(k_ref, v_ref, d_ref, o_ref, v_s, d_s, sem):
    copies = [
        pltpu.make_async_copy(d_ref, d_s.at[0], sem.at[0]),
        pltpu.make_async_copy(v_ref, v_s, sem.at[1]),
        pltpu.make_async_copy(k_ref.at[0:HALF, :], o_ref.at[0:HALF, 0:DEPTH], sem.at[2]),
        pltpu.make_async_copy(
            k_ref.at[HALF:ROWS, :], o_ref.at[0:HALF, DEPTH:HALF], sem.at[3]
        ),
    ]
    for c in copies:
        c.start()
    copies[0].wait()
    d = (d_s[...] + 1).astype(F32)
    o_ref[ROWS:, :] = jnp.concatenate(
        [d[:, 0:HALF], d[:, HALF:ROWS], jnp.zeros((SENT[0] - ROWS - 2, HALF), F32)], axis=0
    ).astype(BF16)
    copies[1].wait()
    vt = v_s[...].T
    o_ref[HALF : HALF + DEPTH, :] = vt[:, 0:HALF]
    o_ref[HALF + DEPTH : ROWS, :] = vt[:, HALF:ROWS]
    for c in copies[2:]:
        c.wait()


def hand(even_ref, odd_ref, after_ref, o_ref):
    core = lax.axis_index("ctx") % 2

    @pl.when(core == 0)
    def _():
        o_ref[...] = even_ref[0 : BLOCK[0], :]

    @pl.when(core == 1)
    def _():
        o_ref[...] = odd_ref[0 : BLOCK[0], :]


def keys(ref, half):
    return ref[0:HALF, half * DEPTH : (half + 1) * DEPTH]


def values(ref, half):
    return ref[HALF + half * DEPTH : HALF + (half + 1) * DEPTH, :]


def docs(ref, half):
    return ref[ROWS : ROWS + 16, :].astype(F32)[half : half + 1, :]


def column(row):
    return jnp.broadcast_to(row, (DEPTH, row.shape[1])).T


def widen(col, lanes):
    return jnp.concatenate([col] * (lanes // DEPTH), axis=1)


def first_doc(own_ref):
    return docs(own_ref, 0)[:, 0:1]


def row_mask(own_ref):
    both = jnp.concatenate([docs(own_ref, 0), docs(own_ref, 1)], axis=1)
    return jnp.where(both == first_doc(own_ref), 1.0, 0.0)


def row_bias(own_ref):
    return (1.0 - row_mask(own_ref)) * NEG


def key_match(own_ref, ref, half):
    return jnp.where(docs(ref, half) == first_doc(own_ref), 1.0, 0.0)


def key_bias(own_ref, ref, half):
    return column((1.0 - key_match(own_ref, ref, half)) * NEG)


def dot(a, b):
    return jnp.dot(a, b, preferred_element_type=F32)


def fold(e):
    return jnp.sum(e.reshape(e.shape[0] // 8, 8, e.shape[1]), axis=0)


def all_keys(ref):
    return jnp.concatenate([keys(ref, 0), keys(ref, 1)], axis=0)


def all_values(ref):
    return jnp.concatenate([values(ref, 0), values(ref, 1)], axis=1)


def head(h):
    return slice(h * DEPTH, (h + 1) * DEPTH)


def eight(h):
    return slice(h * 8, (h + 1) * 8)


def staged(units, first, rest, depth=1):
    held = [first(u) for u in units[:depth]]
    for i, u in enumerate(units):
        if i + depth < len(units):
            held.append(first(units[i + depth]))
        rest(u, held.pop(0))


def triangle(strict):
    key = lax.broadcasted_iota(jnp.int32, (HALF, HALF), 0)
    row = lax.broadcasted_iota(jnp.int32, (HALF, HALF), 1)
    keep = key > row if strict else key <= row
    return jnp.where(keep, 0.0, NEG)


def beside_keys(own_ref, ref):
    both = jnp.concatenate([key_match(own_ref, ref, k) for k in range(2)], axis=1)
    at = lax.broadcasted_iota(jnp.int32, (DEPTH, ROWS), 0)
    rows = jnp.where(at < 64, (1.0 - both) * NEG, 1.0)
    return rows.astype(BF16).T


def below_queries(own_ref):
    at = lax.broadcasted_iota(jnp.int32, (DEPTH, ROWS), 0)
    row = jnp.where(at == 64, row_bias(own_ref), 0.0)
    return jnp.where(at == 0, 1.0, row).astype(BF16)


def full_heads(own_ref, ref, qt_ref, acc_in, sum_in, put, depth):
    kk = jnp.concatenate([all_keys(ref), beside_keys(own_ref, ref)], axis=1)
    vv = all_values(ref)
    below = below_queries(own_ref)

    def first(h):
        return dot(kk, jnp.concatenate([qt_ref[head(h), :], below], axis=0))

    def rest(h, s):
        e = jnp.exp2(s * SCALE)
        o = dot(vv, e.astype(BF16))
        put(h, acc_in[head(h), :] + o, sum_in[eight(h), :] + fold(e))

    staged(range(HEADS), first, rest, depth)


def cut_heads(qt_ref, b_ref, kk, vv, cut, put):
    def first(u):
        h, r = u
        return dot(kk[r], qt_ref[head(h), r * HALF : (r + 1) * HALF])

    def rest(u, s):
        h, r = u
        e = jnp.exp2(s * SCALE + b_ref[cut[r], :])
        put(h, slice(r * HALF, (r + 1) * HALF), dot(vv[r], e.astype(BF16)), fold(e))

    staged([(h, r) for h in range(HEADS) for r in range(2)], first, rest, 2)


def own_block(q_ref, own_ref, qt_ref, acc_ref, sum_ref, b_ref, q_s, sem):
    copies = [
        pltpu.make_async_copy(q_ref.at[:, head(h)], q_s.at[:, head(h)], sem.at[h])
        for h in range(HEADS)
    ]
    for c in copies:
        c.start()
    rows = [docs(own_ref, 0), docs(own_ref, 1)]
    cols = [widen(column(r), HALF) for r in rows]
    apart = lambda k, r: jnp.where(cols[k] == rows[r], 0.0, NEG)
    tri = triangle(False)
    b_ref[0:HALF, :] = apart(0, 1)
    b_ref[HALF:ROWS, :] = apart(1, 1) + tri
    b_ref[ROWS : ROWS + HALF, :] = apart(0, 0) + tri
    for h in range(HEADS):
        copies[h].wait()
        qt_ref[head(h), :] = q_s[:, head(h)].T

    def put(h, cs, o, t):
        acc_ref[head(h), cs] = o
        sum_ref[eight(h), cs] = t

    cut_heads(
        qt_ref,
        b_ref,
        (keys(own_ref, 0), all_keys(own_ref)),
        (values(own_ref, 0), all_values(own_ref)),
        (slice(ROWS, ROWS + HALF), slice(0, ROWS)),
        put,
    )


def full_block(own_ref, ref, qt_ref, acc_in, sum_in, acc_ref, sum_ref):
    def put(h, acc, sums):
        acc_ref[head(h), :] = acc
        sum_ref[eight(h), :] = sums

    full_heads(own_ref, ref, qt_ref, acc_in, sum_in, put, 1)


def far_block(own_ref, ref, qt_ref, acc_in, sum_in, acc_ref, sum_ref, b_ref):
    left, right = slice(0, HALF), slice(HALF, ROWS)

    b_ref[...] = triangle(True)
    beside = beside_keys(own_ref, ref)
    k0 = jnp.concatenate([keys(ref, 0), beside[left, :]], axis=1)
    k1 = jnp.concatenate([keys(ref, 1), beside[right, :]], axis=1)
    below = below_queries(own_ref)

    def first(h):
        q = jnp.concatenate([qt_ref[head(h), :], below], axis=0)
        return dot(k0, q[:, left]), dot(k1, q)

    def rest(h, s):
        s0, s1 = s
        tri = b_ref[...]
        e0 = jnp.exp2(s0 * SCALE + tri)
        cut = jnp.concatenate([s1[:, left] * SCALE, s1[:, right] * SCALE + tri], axis=1)
        e1 = jnp.exp2(cut)
        o1, t1 = dot(values(ref, 1), e1.astype(BF16)), fold(e1)
        o0 = dot(values(ref, 0), e0.astype(BF16)) + o1[:, left]
        t0 = fold(e0) + t1[:, left]
        acc_ref[head(h), left] = acc_in[head(h), left] + o0
        acc_ref[head(h), right] = acc_in[head(h), right] + o1[:, right]
        sum_ref[eight(h), left] = sum_in[eight(h), left] + t0
        sum_ref[eight(h), right] = sum_in[eight(h), right] + t1[:, right]

    staged(range(HEADS), first, rest, 2)


def careful(own_ref, full_refs, far_ref, qt_ref, out_ref, s_ref):
    refs = (own_ref, *full_refs, far_ref)
    lanes = 128
    key0 = lax.broadcasted_iota(jnp.int32, (HALF, lanes), 0)
    row0 = lax.broadcasted_iota(jnp.int32, (HALF, lanes), 1)
    mask = row_mask(own_ref)

    def one(step, carry):
        h, c = step // 4, step % 4
        hs = pl.ds(pl.multiple_of(h * DEPTH, DEPTH), DEPTH)
        cs = pl.ds(pl.multiple_of(c * lanes, lanes), lanes)
        qt = qt_ref[hs, cs]
        row = row0 + c * lanes
        both = [docs(own_ref, r // 2)[:, r % 2 * 128 : r % 2 * 128 + 128] for r in range(4)]
        own_row = mrow = None
        for r in range(4):
            picked = jnp.where(c == r, both[r], 0.0)
            m = jnp.where(c == r, mask[:, r * 128 : (r + 1) * 128], 0.0)
            own_row = picked if own_row is None else own_row + picked
            mrow = m if mrow is None else mrow + m
        for n, ref in enumerate(refs):
            for k in range(2):
                key = key0 + k * HALF
                col = column(docs(ref, k))
                if n == 0:
                    keep = (col == own_row) & (key <= row)
                else:
                    keep = (column(key_match(own_ref, ref, k)) * mrow) > 0.5
                    if ref is far_ref:
                        keep = keep & (key > row)
                s = dot(keys(ref, k), qt) * SCALE
                at = (2 * n + k) * HALF
                s_ref[at : at + HALF, :] = jnp.where(keep, s, NEG)
        top = jnp.max(s_ref[...], axis=0, keepdims=True)
        o, t = jnp.zeros((DEPTH, lanes), F32), jnp.zeros((1, lanes), F32)
        for n, ref in enumerate(refs):
            for k in range(2):
                at = (2 * n + k) * HALF
                e = jnp.exp2(s_ref[at : at + HALF, :] - top)
                t = t + jnp.sum(e, axis=0, keepdims=True)
                o = o + dot(values(ref, k), e.astype(BF16))
        out_ref[cs, hs] = (o / t).T.astype(BF16)
        return carry

    lax.fori_loop(0, HEADS * 4, one, 0)


def last_block(
    own_ref, pa_ref, pb_ref, e1_ref, e2_ref, qt_ref, acc_in, sum_in,
    out_ref, o_s, s_ref, good_ref, sem,
):
    copies = [
        pltpu.make_async_copy(o_s.at[rows, :], out_ref.at[rows, :], sem.at[n])
        for n, rows in enumerate(slice(a, a + 64) for a in range(0, ROWS, 64))
    ]

    def put(h, acc, sums):
        t = jnp.sum(sums, axis=0, keepdims=True)
        good_ref[h : h + 1, :] = jnp.where((t > LOW) & (t < HIGH), 1.0, 0.0)
        o_s[:, head(h)] = (acc * (1.0 / t)).astype(BF16).T

    full_heads(own_ref, e2_ref, qt_ref, acc_in, sum_in, put, 2)
    for c in copies:
        c.start()
    bad = jnp.min(good_ref[...]) < 0.5
    for c in copies:
        c.wait()

    @pl.when(bad)
    def _():
        careful(own_ref, (pa_ref, e1_ref, e2_ref), pb_ref, qt_ref, o_s, s_ref)
        for c in copies:
            c.start()
        for c in copies:
            c.wait()


def local(queries, k, v, doc_ids):
    size = lax.axis_size("ctx")
    block = jax.ShapeDtypeStruct(BLOCK, BF16)
    qt_out = jax.ShapeDtypeStruct(QT, BF16)
    acc_out = jax.ShapeDtypeStruct(QT, F32)
    sum_out = jax.ShapeDtypeStruct(SUMS, F32)
    dma = pltpu.SemaphoreType.DMA

    def move(x, pairs):
        return lax.ppermute(x, "ctx", [(a, b) for a, b in pairs if 0 <= b < size])

    own = call(
        pack,
        jax.ShapeDtypeStruct(SENT, BF16),
        (ANY, ANY, ANY),
        scratch=(
            pltpu.VMEM((ROWS, DEPTH), BF16),
            pltpu.VMEM((1, ROWS), jnp.int32),
            dma((4,)),
        ),
    )(in_hbm(k), in_hbm(v), in_hbm(doc_ids))
    pa = move(own, [(i, i + (1 if i % 2 else 3)) for i in range(size)])
    pb = move(own, [(i, i + 4) for i in range(size)])
    qt, acc, sums = call(
        own_block,
        (qt_out, acc_out, sum_out),
        (ANY, VM),
        scratch=(BIAS, pltpu.VMEM((ROWS, HEADS * DEPTH), BF16), dma((HEADS,))),
    )(in_hbm(queries), own)
    swap = [(i, i ^ 1) for i in range(size)]
    hand_over = call(hand, block, (VM, VM, ANY))
    full = call(full_block, (acc_out, sum_out))
    e1 = move(hand_over(own, pb, sums), swap)
    acc, sums = call(far_block, (acc_out, sum_out), scratch=(TRI,))(
        own, pb, qt, acc, sums
    )
    acc, sums = full(own, e1, qt, acc, sums)
    e2 = move(hand_over(pa, pa, sums), swap)
    acc, sums = full(own, pa, qt, acc, sums)
    return call(
        last_block,
        jax.ShapeDtypeStruct(queries.shape, BF16),
        outs=ANY,
        scratch=(
            pltpu.VMEM((ROWS, HEADS * DEPTH), BF16),
            pltpu.VMEM((10 * HALF, 128), F32),
            pltpu.VMEM((HEADS, ROWS), F32),
            dma((8,)),
        ),
    )(own, pa, pb, e1, e2, qt, acc, sums)


def solution(mesh):
    return jax.shard_map(
        local,
        mesh=mesh,
        in_specs=(P("ctx", None), P("ctx", None), P("ctx", None), P("ctx")),
        out_specs=P("ctx", None),
        check_vma=False,
    )
```

```python
import jax
import jax.numpy as jnp
from jax import lax
from jax.experimental import pallas as pl
from jax.experimental.pallas import tpu as pltpu
from jax.sharding import PartitionSpec as P

ROWS = 512
HALF = 256
DEPTH = 128
HEADS = 8
SCALE = 1.4426950408889634 / DEPTH**0.5
NEG = -1e30
LOW, HIGH = 2.0**-60, 2.0**100
VM = pl.BlockSpec(memory_space=pltpu.VMEM)
SENT = (2 * ROWS + 32, DEPTH)
BLOCK = (2 * ROWS + 16, DEPTH)
QT = (HEADS * DEPTH, ROWS)
SUMS = (HEADS * 8, ROWS)
F32 = jnp.float32
BF16 = jnp.bfloat16


ANY = pl.BlockSpec(memory_space=pl.ANY)
BIAS = pltpu.VMEM((ROWS + HALF, HALF), F32)
TRI = pltpu.VMEM((HALF, HALF), F32)


def call(body, out, ins=None, outs=None, scratch=()):
    return pl.pallas_call(
        body,
        out_shape=out,
        **({} if ins is None else {"in_specs": ins}),
        out_specs=outs or jax.tree.map(lambda _: VM, out),
        scratch_shapes=scratch,
        cost_estimate=pl.CostEstimate(flops=1, bytes_accessed=1, transcendentals=0),
        compiler_params=pltpu.CompilerParams(vmem_limit_bytes=16 << 20),
    )


def in_hbm(x):
    return pltpu.with_memory_space_constraint(x, pltpu.HBM)


def pack(k_ref, v_ref, d_ref, o_ref, v_s, d_s, sem):
    copies = [
        pltpu.make_async_copy(v_ref, v_s, sem.at[0]),
        pltpu.make_async_copy(d_ref, d_s.at[0], sem.at[1]),
        pltpu.make_async_copy(k_ref, o_ref.at[0:ROWS, :], sem.at[2]),
    ]
    for c in copies:
        c.start()
    copies[1].wait()
    d = (d_s[...] + 1).astype(F32)
    rows = [d[:, a : a + DEPTH] for a in range(0, ROWS, DEPTH)]
    pad = jnp.zeros((SENT[0] - 2 * ROWS - 4, DEPTH), F32)
    o_ref[2 * ROWS :, :] = jnp.concatenate([*rows, pad], axis=0).astype(BF16)
    copies[0].wait()
    for a in range(0, ROWS, DEPTH):
        o_ref[ROWS + a : ROWS + a + DEPTH, :] = v_s[a : a + DEPTH, :].T
    copies[2].wait()


def hand(even_ref, odd_ref, after_ref, o_ref):
    core = lax.axis_index("ctx") % 2

    @pl.when(core == 0)
    def _():
        o_ref[...] = even_ref[0 : BLOCK[0], :]

    @pl.when(core == 1)
    def _():
        o_ref[...] = odd_ref[0 : BLOCK[0], :]


def keys(ref, half):
    return ref[half * HALF : (half + 1) * HALF, :]


def values(ref, half):
    at = ROWS + half * HALF
    return jnp.concatenate(
        [ref[at : at + DEPTH, :], ref[at + DEPTH : at + 2 * DEPTH, :]], axis=1
    )


def docs(ref, half):
    rows = ref[2 * ROWS : 2 * ROWS + 16, :].astype(F32)
    return jnp.concatenate(
        [rows[2 * half : 2 * half + 1, :], rows[2 * half + 1 : 2 * half + 2, :]], axis=1
    )


def column(row):
    return jnp.broadcast_to(row, (DEPTH, row.shape[1])).T


def widen(col, lanes):
    return jnp.concatenate([col] * (lanes // DEPTH), axis=1)


def first_doc(own_ref):
    return docs(own_ref, 0)[:, 0:1]


def row_mask(own_ref):
    both = jnp.concatenate([docs(own_ref, 0), docs(own_ref, 1)], axis=1)
    return jnp.where(both == first_doc(own_ref), 1.0, 0.0)


def row_bias(own_ref):
    return (1.0 - row_mask(own_ref)) * NEG


def key_match(own_ref, ref, half):
    return jnp.where(docs(ref, half) == first_doc(own_ref), 1.0, 0.0)


def key_bias(own_ref, ref, half):
    return column((1.0 - key_match(own_ref, ref, half)) * NEG)


def dot(a, b):
    return jnp.dot(a, b, preferred_element_type=F32)


def fold(e):
    return jnp.sum(e.reshape(e.shape[0] // 8, 8, e.shape[1]), axis=0)


def all_keys(ref):
    return ref[0:ROWS, :]


def all_values(ref):
    return jnp.concatenate([values(ref, 0), values(ref, 1)], axis=1)


def head(h):
    return slice(h * DEPTH, (h + 1) * DEPTH)


def eight(h):
    return slice(h * 8, (h + 1) * 8)


def staged(units, first, rest, depth=1):
    held = [first(u) for u in units[:depth]]
    for i, u in enumerate(units):
        if i + depth < len(units):
            held.append(first(units[i + depth]))
        rest(u, held.pop(0))


def triangle(strict):
    key = lax.broadcasted_iota(jnp.int32, (HALF, HALF), 0)
    row = lax.broadcasted_iota(jnp.int32, (HALF, HALF), 1)
    keep = key > row if strict else key <= row
    return jnp.where(keep, 0.0, NEG)


def beside_keys(own_ref, ref):
    both = jnp.concatenate([key_match(own_ref, ref, k) for k in range(2)], axis=1)
    at = lax.broadcasted_iota(jnp.int32, (DEPTH, ROWS), 0)
    rows = jnp.where(at < 64, (1.0 - both) * NEG, 1.0)
    return rows.astype(BF16).T


def below_queries(own_ref):
    at = lax.broadcasted_iota(jnp.int32, (DEPTH, ROWS), 0)
    row = jnp.where(at == 64, row_bias(own_ref), 0.0)
    return jnp.where(at == 0, 1.0, row).astype(BF16)


def full_heads(own_ref, ref, qt_ref, acc_in, sum_in, put, depth):
    kk = jnp.concatenate([all_keys(ref), beside_keys(own_ref, ref)], axis=1)
    vv = all_values(ref)
    below = below_queries(own_ref)

    def first(h):
        return dot(kk, jnp.concatenate([qt_ref[head(h), :], below], axis=0))

    def rest(h, s):
        e = jnp.exp2(s * SCALE)
        o = dot(vv, e.astype(BF16))
        put(h, acc_in[head(h), :] + o, sum_in[eight(h), :] + fold(e))

    staged(range(HEADS), first, rest, depth)


def cut_heads(qt_ref, b_ref, kk, vv, cut, put):
    def first(u):
        h, r = u
        return dot(kk[r], qt_ref[head(h), r * HALF : (r + 1) * HALF])

    def rest(u, s):
        h, r = u
        e = jnp.exp2(s * SCALE + b_ref[cut[r], :])
        put(h, slice(r * HALF, (r + 1) * HALF), dot(vv[r], e.astype(BF16)), fold(e))

    staged([(h, r) for h in range(HEADS) for r in range(2)], first, rest, 2)


def own_block(q_ref, own_ref, qt_ref, acc_ref, sum_ref, b_ref, q_s, sem):
    copies = [
        pltpu.make_async_copy(q_ref.at[:, head(h)], q_s.at[:, head(h)], sem.at[h])
        for h in range(HEADS)
    ]
    for c in copies:
        c.start()
    rows = [docs(own_ref, 0), docs(own_ref, 1)]
    cols = [widen(column(r), HALF) for r in rows]
    apart = lambda k, r: jnp.where(cols[k] == rows[r], 0.0, NEG)
    tri = triangle(False)
    b_ref[0:HALF, :] = apart(0, 1)
    b_ref[HALF:ROWS, :] = apart(1, 1) + tri
    b_ref[ROWS : ROWS + HALF, :] = apart(0, 0) + tri
    for h in range(HEADS):
        copies[h].wait()
        qt_ref[head(h), :] = q_s[:, head(h)].T

    def put(h, cs, o, t):
        acc_ref[head(h), cs] = o
        sum_ref[eight(h), cs] = t

    cut_heads(
        qt_ref,
        b_ref,
        (keys(own_ref, 0), all_keys(own_ref)),
        (values(own_ref, 0), all_values(own_ref)),
        (slice(ROWS, ROWS + HALF), slice(0, ROWS)),
        put,
    )


def full_block(own_ref, ref, qt_ref, acc_in, sum_in, acc_ref, sum_ref):
    def put(h, acc, sums):
        acc_ref[head(h), :] = acc
        sum_ref[eight(h), :] = sums

    full_heads(own_ref, ref, qt_ref, acc_in, sum_in, put, 1)


def far_block(own_ref, ref, qt_ref, acc_in, sum_in, acc_ref, sum_ref, b_ref):
    left, right = slice(0, HALF), slice(HALF, ROWS)

    b_ref[...] = triangle(True)
    beside = beside_keys(own_ref, ref)
    k0 = jnp.concatenate([keys(ref, 0), beside[left, :]], axis=1)
    k1 = jnp.concatenate([keys(ref, 1), beside[right, :]], axis=1)
    below = below_queries(own_ref)

    def first(h):
        q = jnp.concatenate([qt_ref[head(h), :], below], axis=0)
        return dot(k0, q[:, left]), dot(k1, q)

    def rest(h, s):
        s0, s1 = s
        tri = b_ref[...]
        e0 = jnp.exp2(s0 * SCALE + tri)
        cut = jnp.concatenate([s1[:, left] * SCALE, s1[:, right] * SCALE + tri], axis=1)
        e1 = jnp.exp2(cut)
        o1, t1 = dot(values(ref, 1), e1.astype(BF16)), fold(e1)
        o0 = dot(values(ref, 0), e0.astype(BF16)) + o1[:, left]
        t0 = fold(e0) + t1[:, left]
        acc_ref[head(h), left] = acc_in[head(h), left] + o0
        acc_ref[head(h), right] = acc_in[head(h), right] + o1[:, right]
        sum_ref[eight(h), left] = sum_in[eight(h), left] + t0
        sum_ref[eight(h), right] = sum_in[eight(h), right] + t1[:, right]

    staged(range(HEADS), first, rest, 2)


def careful(own_ref, full_refs, far_ref, qt_ref, out_ref, s_ref):
    refs = (own_ref, *full_refs, far_ref)
    lanes = 128
    key0 = lax.broadcasted_iota(jnp.int32, (HALF, lanes), 0)
    row0 = lax.broadcasted_iota(jnp.int32, (HALF, lanes), 1)
    mask = row_mask(own_ref)

    def one(step, carry):
        h, c = step // 4, step % 4
        hs = pl.ds(pl.multiple_of(h * DEPTH, DEPTH), DEPTH)
        cs = pl.ds(pl.multiple_of(c * lanes, lanes), lanes)
        qt = qt_ref[hs, cs]
        row = row0 + c * lanes
        both = [docs(own_ref, r // 2)[:, r % 2 * 128 : r % 2 * 128 + 128] for r in range(4)]
        own_row = mrow = None
        for r in range(4):
            picked = jnp.where(c == r, both[r], 0.0)
            m = jnp.where(c == r, mask[:, r * 128 : (r + 1) * 128], 0.0)
            own_row = picked if own_row is None else own_row + picked
            mrow = m if mrow is None else mrow + m
        for n, ref in enumerate(refs):
            for k in range(2):
                key = key0 + k * HALF
                col = column(docs(ref, k))
                if n == 0:
                    keep = (col == own_row) & (key <= row)
                else:
                    keep = (column(key_match(own_ref, ref, k)) * mrow) > 0.5
                    if ref is far_ref:
                        keep = keep & (key > row)
                s = dot(keys(ref, k), qt) * SCALE
                at = (2 * n + k) * HALF
                s_ref[at : at + HALF, :] = jnp.where(keep, s, NEG)
        top = jnp.max(s_ref[...], axis=0, keepdims=True)
        o, t = jnp.zeros((DEPTH, lanes), F32), jnp.zeros((1, lanes), F32)
        for n, ref in enumerate(refs):
            for k in range(2):
                at = (2 * n + k) * HALF
                e = jnp.exp2(s_ref[at : at + HALF, :] - top)
                t = t + jnp.sum(e, axis=0, keepdims=True)
                o = o + dot(values(ref, k), e.astype(BF16))
        out_ref[cs, hs] = (o / t).T.astype(BF16)
        return carry

    lax.fori_loop(0, HEADS * 4, one, 0)


def last_block(
    own_ref, pa_ref, pb_ref, e1_ref, e2_ref, qt_ref, acc_in, sum_in,
    out_ref, o_s, s_ref, good_ref, sem,
):
    copies = [
        pltpu.make_async_copy(o_s.at[rows, :], out_ref.at[rows, :], sem.at[n])
        for n, rows in enumerate(slice(a, a + 128) for a in range(0, ROWS, 128))
    ]

    def put(h, acc, sums):
        t = jnp.sum(sums, axis=0, keepdims=True)
        good_ref[h : h + 1, :] = jnp.where((t > LOW) & (t < HIGH), 1.0, 0.0)
        o_s[:, head(h)] = (acc * (1.0 / t)).astype(BF16).T

    full_heads(own_ref, e2_ref, qt_ref, acc_in, sum_in, put, 2)
    for c in copies:
        c.start()
    bad = jnp.min(good_ref[...]) < 0.5
    for c in copies:
        c.wait()

    @pl.when(bad)
    def _():
        careful(own_ref, (pa_ref, e1_ref, e2_ref), pb_ref, qt_ref, o_s, s_ref)
        for c in copies:
            c.start()
        for c in copies:
            c.wait()


def local(queries, k, v, doc_ids):
    size = lax.axis_size("ctx")
    block = jax.ShapeDtypeStruct(BLOCK, BF16)
    qt_out = jax.ShapeDtypeStruct(QT, BF16)
    acc_out = jax.ShapeDtypeStruct(QT, F32)
    sum_out = jax.ShapeDtypeStruct(SUMS, F32)
    dma = pltpu.SemaphoreType.DMA

    def move(x, pairs):
        return lax.ppermute(x, "ctx", [(a, b) for a, b in pairs if 0 <= b < size])

    own = call(
        pack,
        jax.ShapeDtypeStruct(SENT, BF16),
        (ANY, ANY, ANY),
        scratch=(
            pltpu.VMEM((ROWS, DEPTH), BF16),
            pltpu.VMEM((1, ROWS), jnp.int32),
            dma((3,)),
        ),
    )(in_hbm(k), in_hbm(v), in_hbm(doc_ids))
    pa = move(own, [(i, i + (1 if i % 2 else 3)) for i in range(size)])
    pb = move(own, [(i, i + 4) for i in range(size)])
    qt, acc, sums = call(
        own_block,
        (qt_out, acc_out, sum_out),
        (ANY, VM),
        scratch=(BIAS, pltpu.VMEM((ROWS, HEADS * DEPTH), BF16), dma((HEADS,))),
    )(in_hbm(queries), own)
    swap = [(i, i ^ 1) for i in range(size)]
    hand_over = call(hand, block, (VM, VM, ANY))
    full = call(full_block, (acc_out, sum_out))
    e1 = move(hand_over(own, pb, sums), swap)
    acc, sums = call(far_block, (acc_out, sum_out), scratch=(TRI,))(
        own, pb, qt, acc, sums
    )
    acc, sums = full(own, e1, qt, acc, sums)
    e2 = move(hand_over(pa, pa, sums), swap)
    acc, sums = full(own, pa, qt, acc, sums)
    return call(
        last_block,
        jax.ShapeDtypeStruct(queries.shape, BF16),
        outs=ANY,
        scratch=(
            pltpu.VMEM((ROWS, HEADS * DEPTH), BF16),
            pltpu.VMEM((10 * HALF, 128), F32),
            pltpu.VMEM((HEADS, ROWS), F32),
            dma((4,)),
        ),
    )(own, pa, pb, e1, e2, qt, acc, sums)


def solution(mesh):
    return jax.shard_map(
        local,
        mesh=mesh,
        in_specs=(P("ctx", None), P("ctx", None), P("ctx", None), P("ctx")),
        out_specs=P("ctx", None),
        check_vma=False,
    )
```

```python
import jax
import jax.numpy as jnp
from jax import lax
from jax.experimental import pallas as pl
from jax.experimental.pallas import tpu as pltpu
from jax.sharding import PartitionSpec as P

ROWS = 512
HALF = 256
DEPTH = 128
HEADS = 8
SCALE = 1.4426950408889634 / DEPTH**0.5
NEG = -1e30
LOW, HIGH = 2.0**-60, 2.0**100
VM = pl.BlockSpec(memory_space=pltpu.VMEM)
SENT = (2 * ROWS + 32, DEPTH)
BLOCK = (2 * ROWS + 16, DEPTH)
QT = (HEADS * DEPTH, ROWS)
SUMS = (HEADS * 8, ROWS)
F32 = jnp.float32
BF16 = jnp.bfloat16


ANY = pl.BlockSpec(memory_space=pl.ANY)
BIAS = pltpu.VMEM((ROWS + HALF, HALF), F32)
TRI = pltpu.VMEM((HALF, HALF), F32)


def call(body, out, ins=None, outs=None, scratch=()):
    return pl.pallas_call(
        body,
        out_shape=out,
        **({} if ins is None else {"in_specs": ins}),
        out_specs=outs or jax.tree.map(lambda _: VM, out),
        scratch_shapes=scratch,
        cost_estimate=pl.CostEstimate(flops=1, bytes_accessed=1, transcendentals=0),
        compiler_params=pltpu.CompilerParams(vmem_limit_bytes=16 << 20),
    )


def in_hbm(x):
    return pltpu.with_memory_space_constraint(x, pltpu.HBM)


def pack(k_ref, v_ref, d_ref, o_ref, v_s, d_s, sem):
    copies = [
        pltpu.make_async_copy(v_ref, v_s, sem.at[0]),
        pltpu.make_async_copy(d_ref, d_s.at[0], sem.at[1]),
        pltpu.make_async_copy(k_ref, o_ref.at[0:ROWS, :], sem.at[2]),
    ]
    for c in copies:
        c.start()
    copies[1].wait()
    d = (d_s[...] + 1).astype(F32)
    rows = [d[:, a : a + DEPTH] for a in range(0, ROWS, DEPTH)]
    pad = jnp.zeros((SENT[0] - 2 * ROWS - 4, DEPTH), F32)
    o_ref[2 * ROWS :, :] = jnp.concatenate([*rows, pad], axis=0).astype(BF16)
    copies[0].wait()
    for a in range(0, ROWS, DEPTH):
        o_ref[ROWS + a : ROWS + a + DEPTH, :] = v_s[a : a + DEPTH, :].T
    copies[2].wait()


def hand(even_ref, odd_ref, after_ref, o_ref):
    core = lax.axis_index("ctx") % 2

    @pl.when(core == 0)
    def _():
        o_ref[...] = even_ref[0 : BLOCK[0], :]

    @pl.when(core == 1)
    def _():
        o_ref[...] = odd_ref[0 : BLOCK[0], :]


def keys(ref, half):
    return ref[half * HALF : (half + 1) * HALF, :]


def values(ref, half):
    at = ROWS + half * HALF
    return jnp.concatenate(
        [ref[at : at + DEPTH, :], ref[at + DEPTH : at + 2 * DEPTH, :]], axis=1
    )


def docs(ref, half):
    rows = ref[2 * ROWS : 2 * ROWS + 16, :].astype(F32)
    return jnp.concatenate(
        [rows[2 * half : 2 * half + 1, :], rows[2 * half + 1 : 2 * half + 2, :]], axis=1
    )


def column(row):
    return jnp.broadcast_to(row, (DEPTH, row.shape[1])).T


def widen(col, lanes):
    return jnp.concatenate([col] * (lanes // DEPTH), axis=1)


def first_doc(own_ref):
    return docs(own_ref, 0)[:, 0:1]


def row_mask(own_ref):
    both = jnp.concatenate([docs(own_ref, 0), docs(own_ref, 1)], axis=1)
    return jnp.where(both == first_doc(own_ref), 1.0, 0.0)


def row_bias(own_ref):
    return (1.0 - row_mask(own_ref)) * NEG


def key_match(own_ref, ref, half):
    return jnp.where(docs(ref, half) == first_doc(own_ref), 1.0, 0.0)


def key_bias(own_ref, ref, half):
    return column((1.0 - key_match(own_ref, ref, half)) * NEG)


def dot(a, b):
    return jnp.dot(a, b, preferred_element_type=F32)


def fold(e):
    return jnp.sum(e.reshape(e.shape[0] // 8, 8, e.shape[1]), axis=0)


def all_keys(ref):
    return ref[0:ROWS, :]


def all_values(ref):
    return jnp.concatenate([values(ref, 0), values(ref, 1)], axis=1)


def head(h):
    return slice(h * DEPTH, (h + 1) * DEPTH)


def eight(h):
    return slice(h * 8, (h + 1) * 8)


def staged(units, first, rest, depth=1):
    held = [first(u) for u in units[:depth]]
    for i, u in enumerate(units):
        if i + depth < len(units):
            held.append(first(units[i + depth]))
        rest(u, held.pop(0))


def triangle(strict):
    key = lax.broadcasted_iota(jnp.int32, (HALF, HALF), 0)
    row = lax.broadcasted_iota(jnp.int32, (HALF, HALF), 1)
    keep = key > row if strict else key <= row
    return jnp.where(keep, 0.0, NEG)


def beside_keys(own_ref, ref):
    both = jnp.concatenate([key_match(own_ref, ref, k) for k in range(2)], axis=1)
    at = lax.broadcasted_iota(jnp.int32, (DEPTH, ROWS), 0)
    rows = jnp.where(at < 64, (1.0 - both) * NEG, 1.0)
    return rows.astype(BF16).T


def below_queries(own_ref):
    at = lax.broadcasted_iota(jnp.int32, (DEPTH, ROWS), 0)
    row = jnp.where(at == 64, row_bias(own_ref), 0.0)
    return jnp.where(at == 0, 1.0, row).astype(BF16)


def full_heads(own_ref, ref, qt_ref, acc_in, sum_in, put, depth):
    kk = jnp.concatenate([all_keys(ref), beside_keys(own_ref, ref)], axis=1)
    vv = all_values(ref)
    below = below_queries(own_ref)

    def first(h):
        return dot(kk, jnp.concatenate([qt_ref[head(h), :], below], axis=0))

    def rest(h, s):
        e = jnp.exp2(s * SCALE)
        o = dot(vv, e.astype(BF16))
        put(h, acc_in[head(h), :] + o, sum_in[eight(h), :] + fold(e))

    staged(range(HEADS), first, rest, depth)


def cut_heads(qt_ref, b_ref, kk, vv, cut, put):
    def first(u):
        h, r = u
        return dot(kk[r], qt_ref[head(h), r * HALF : (r + 1) * HALF])

    def rest(u, s):
        h, r = u
        e = jnp.exp2(s * SCALE + b_ref[cut[r], :])
        put(h, slice(r * HALF, (r + 1) * HALF), dot(vv[r], e.astype(BF16)), fold(e))

    staged([(h, r) for h in range(HEADS) for r in range(2)], first, rest, 2)


def own_block(q_ref, own_ref, qt_ref, acc_ref, sum_ref, b_ref, q_s, sem):
    copies = [
        pltpu.make_async_copy(q_ref.at[:, head(h)], q_s.at[:, head(h)], sem.at[h])
        for h in range(HEADS)
    ]
    for c in copies:
        c.start()
    rows = [docs(own_ref, 0), docs(own_ref, 1)]
    cols = [widen(column(r), HALF) for r in rows]
    apart = lambda k, r: jnp.where(cols[k] == rows[r], 0.0, NEG)
    tri = triangle(False)
    b_ref[0:HALF, :] = apart(0, 1)
    b_ref[HALF:ROWS, :] = apart(1, 1) + tri
    b_ref[ROWS : ROWS + HALF, :] = apart(0, 0) + tri
    for h in range(HEADS):
        copies[h].wait()
        qt_ref[head(h), :] = q_s[:, head(h)].T

    def put(h, cs, o, t):
        acc_ref[head(h), cs] = o
        sum_ref[eight(h), cs] = t

    cut_heads(
        qt_ref,
        b_ref,
        (keys(own_ref, 0), all_keys(own_ref)),
        (values(own_ref, 0), all_values(own_ref)),
        (slice(ROWS, ROWS + HALF), slice(0, ROWS)),
        put,
    )


def full_block(own_ref, ref, qt_ref, acc_in, sum_in, acc_ref, sum_ref):
    def put(h, acc, sums):
        acc_ref[head(h), :] = acc
        sum_ref[eight(h), :] = sums

    full_heads(own_ref, ref, qt_ref, acc_in, sum_in, put, 1)


def far_block(own_ref, ref, qt_ref, acc_in, sum_in, acc_ref, sum_ref, b_ref):
    left, right = slice(0, HALF), slice(HALF, ROWS)

    b_ref[...] = triangle(True)
    beside = beside_keys(own_ref, ref)
    k0 = jnp.concatenate([keys(ref, 0), beside[left, :]], axis=1)
    k1 = jnp.concatenate([keys(ref, 1), beside[right, :]], axis=1)
    below = below_queries(own_ref)

    def first(h):
        q = jnp.concatenate([qt_ref[head(h), :], below], axis=0)
        return dot(k0, q[:, left]), dot(k1, q)

    def rest(h, s):
        s0, s1 = s
        tri = b_ref[...]
        e0 = jnp.exp2(s0 * SCALE + tri)
        cut = jnp.concatenate([s1[:, left] * SCALE, s1[:, right] * SCALE + tri], axis=1)
        e1 = jnp.exp2(cut)
        o1, t1 = dot(values(ref, 1), e1.astype(BF16)), fold(e1)
        o0 = dot(values(ref, 0), e0.astype(BF16)) + o1[:, left]
        t0 = fold(e0) + t1[:, left]
        acc_ref[head(h), left] = acc_in[head(h), left] + o0
        acc_ref[head(h), right] = acc_in[head(h), right] + o1[:, right]
        sum_ref[eight(h), left] = sum_in[eight(h), left] + t0
        sum_ref[eight(h), right] = sum_in[eight(h), right] + t1[:, right]

    staged(range(HEADS), first, rest, 2)


def careful(own_ref, full_refs, far_ref, qt_ref, out_ref, s_ref):
    refs = (own_ref, *full_refs, far_ref)
    lanes = 128
    key0 = lax.broadcasted_iota(jnp.int32, (HALF, lanes), 0)
    row0 = lax.broadcasted_iota(jnp.int32, (HALF, lanes), 1)
    mask = row_mask(own_ref)

    def one(step, carry):
        h, c = step // 4, step % 4
        hs = pl.ds(pl.multiple_of(h * DEPTH, DEPTH), DEPTH)
        cs = pl.ds(pl.multiple_of(c * lanes, lanes), lanes)
        qt = qt_ref[hs, cs]
        row = row0 + c * lanes
        both = [docs(own_ref, r // 2)[:, r % 2 * 128 : r % 2 * 128 + 128] for r in range(4)]
        own_row = mrow = None
        for r in range(4):
            picked = jnp.where(c == r, both[r], 0.0)
            m = jnp.where(c == r, mask[:, r * 128 : (r + 1) * 128], 0.0)
            own_row = picked if own_row is None else own_row + picked
            mrow = m if mrow is None else mrow + m
        for n, ref in enumerate(refs):
            for k in range(2):
                key = key0 + k * HALF
                col = column(docs(ref, k))
                if n == 0:
                    keep = (col == own_row) & (key <= row)
                else:
                    keep = (column(key_match(own_ref, ref, k)) * mrow) > 0.5
                    if ref is far_ref:
                        keep = keep & (key > row)
                s = dot(keys(ref, k), qt) * SCALE
                at = (2 * n + k) * HALF
                s_ref[at : at + HALF, :] = jnp.where(keep, s, NEG)
        top = jnp.max(s_ref[...], axis=0, keepdims=True)
        o, t = jnp.zeros((DEPTH, lanes), F32), jnp.zeros((1, lanes), F32)
        for n, ref in enumerate(refs):
            for k in range(2):
                at = (2 * n + k) * HALF
                e = jnp.exp2(s_ref[at : at + HALF, :] - top)
                t = t + jnp.sum(e, axis=0, keepdims=True)
                o = o + dot(values(ref, k), e.astype(BF16))
        out_ref[cs, hs] = (o / t).T.astype(BF16)
        return carry

    lax.fori_loop(0, HEADS * 4, one, 0)


def last_block(
    own_ref, pa_ref, pb_ref, e1_ref, e2_ref, qt_ref, acc_in, sum_in,
    out_ref, o_s, s_ref, good_ref, sem,
):
    copies = [
        pltpu.make_async_copy(o_s.at[rows, :], out_ref.at[rows, :], sem.at[n])
        for n, rows in enumerate(slice(a, a + 128) for a in range(0, ROWS, 128))
    ]

    def put(h, acc, sums):
        t = jnp.sum(sums, axis=0, keepdims=True)
        good_ref[h : h + 1, :] = jnp.where((t > LOW) & (t < HIGH), 1.0, 0.0)
        o_s[:, head(h)] = (acc * (1.0 / t)).astype(BF16).T

    full_heads(own_ref, e2_ref, qt_ref, acc_in, sum_in, put, 2)
    for c in copies:
        c.start()
    bad = jnp.min(good_ref[...]) < 0.5
    for c in copies:
        c.wait()

    @pl.when(bad)
    def _():
        careful(own_ref, (pa_ref, e1_ref, e2_ref), pb_ref, qt_ref, o_s, s_ref)
        for c in copies:
            c.start()
        for c in copies:
            c.wait()


def local(queries, k, v, doc_ids):
    size = lax.axis_size("ctx")
    block = jax.ShapeDtypeStruct(BLOCK, BF16)
    qt_out = jax.ShapeDtypeStruct(QT, BF16)
    acc_out = jax.ShapeDtypeStruct(QT, F32)
    sum_out = jax.ShapeDtypeStruct(SUMS, F32)
    dma = pltpu.SemaphoreType.DMA

    def move(x, pairs):
        return lax.ppermute(x, "ctx", [(a, b) for a, b in pairs if 0 <= b < size])

    own = call(
        pack,
        jax.ShapeDtypeStruct(SENT, BF16),
        (ANY, ANY, ANY),
        scratch=(
            pltpu.VMEM((ROWS, DEPTH), BF16),
            pltpu.VMEM((1, ROWS), jnp.int32),
            dma((3,)),
        ),
    )(in_hbm(k), in_hbm(v), in_hbm(doc_ids))
    pa = move(own, [(i, i + 2) for i in range(size)])
    pb = move(own, [(i, i + 4) for i in range(size)])
    qt, acc, sums = call(
        own_block,
        (qt_out, acc_out, sum_out),
        (ANY, VM),
        scratch=(BIAS, pltpu.VMEM((ROWS, HEADS * DEPTH), BF16), dma((HEADS,))),
    )(in_hbm(queries), own)
    swap = [(i, i ^ 1) for i in range(size)]
    hand_over = call(hand, block, (VM, VM, ANY))
    full = call(full_block, (acc_out, sum_out))
    e1 = move(hand_over(own, pb, sums), swap)
    acc, sums = call(far_block, (acc_out, sum_out), scratch=(TRI,))(
        own, pb, qt, acc, sums
    )
    acc, sums = full(own, e1, qt, acc, sums)
    e2 = move(hand_over(pa, pa, sums), swap)
    acc, sums = full(own, pa, qt, acc, sums)
    return call(
        last_block,
        jax.ShapeDtypeStruct(queries.shape, BF16),
        outs=ANY,
        scratch=(
            pltpu.VMEM((ROWS, HEADS * DEPTH), BF16),
            pltpu.VMEM((10 * HALF, 128), F32),
            pltpu.VMEM((HEADS, ROWS), F32),
            dma((4,)),
        ),
    )(own, pa, pb, e1, e2, qt, acc, sums)


def solution(mesh):
    return jax.shard_map(
        local,
        mesh=mesh,
        in_specs=(P("ctx", None), P("ctx", None), P("ctx", None), P("ctx")),
        out_specs=P("ctx", None),
        check_vma=False,
    )
```

```python
import jax
import jax.numpy as jnp
from jax import lax
from jax.experimental import pallas as pl
from jax.experimental.pallas import tpu as pltpu
from jax.sharding import PartitionSpec as P

ROWS = 512
HALF = 256
DEPTH = 128
HEADS = 8
SCALE = 1.4426950408889634 / DEPTH**0.5
NEG = -1e30
LOW, HIGH = 2.0**-60, 2.0**100
VM = pl.BlockSpec(memory_space=pltpu.VMEM)
SENT = (2 * ROWS + 32, DEPTH)
BLOCK = (2 * ROWS + 16, DEPTH)
QT = (HEADS * DEPTH, ROWS)
SUMS = (HEADS * 8, ROWS)
F32 = jnp.float32
BF16 = jnp.bfloat16


ANY = pl.BlockSpec(memory_space=pl.ANY)
BIAS = pltpu.VMEM((ROWS + HALF, HALF), F32)
TRI = pltpu.VMEM((HALF, HALF), F32)


def call(body, out, ins=None, outs=None, scratch=()):
    return pl.pallas_call(
        body,
        out_shape=out,
        **({} if ins is None else {"in_specs": ins}),
        out_specs=outs or jax.tree.map(lambda _: VM, out),
        scratch_shapes=scratch,
        cost_estimate=pl.CostEstimate(flops=1, bytes_accessed=1, transcendentals=0),
        compiler_params=pltpu.CompilerParams(vmem_limit_bytes=16 << 20),
    )


def in_hbm(x):
    return pltpu.with_memory_space_constraint(x, pltpu.HBM)


def pack(k_ref, v_ref, d_ref, o_ref, v_s, d_s, sem):
    copies = [
        pltpu.make_async_copy(v_ref, v_s, sem.at[0]),
        pltpu.make_async_copy(d_ref, d_s.at[0], sem.at[1]),
        pltpu.make_async_copy(k_ref, o_ref.at[0:ROWS, :], sem.at[2]),
    ]
    for c in copies:
        c.start()
    copies[1].wait()
    d = (d_s[...] + 1).astype(F32)
    rows = [d[:, a : a + DEPTH] for a in range(0, ROWS, DEPTH)]
    pad = jnp.zeros((SENT[0] - 2 * ROWS - 4, DEPTH), F32)
    o_ref[2 * ROWS :, :] = jnp.concatenate([*rows, pad], axis=0).astype(BF16)
    copies[0].wait()
    for a in range(0, ROWS, DEPTH):
        o_ref[ROWS + a : ROWS + a + DEPTH, :] = v_s[a : a + DEPTH, :].T
    copies[2].wait()


def hand(even_ref, odd_ref, after_ref, o_ref):
    core = lax.axis_index("ctx") % 2

    @pl.when(core == 0)
    def _():
        o_ref[...] = even_ref[0 : BLOCK[0], :]

    @pl.when(core == 1)
    def _():
        o_ref[...] = odd_ref[0 : BLOCK[0], :]


def keys(ref, half):
    return ref[half * HALF : (half + 1) * HALF, :]


def values(ref, half):
    at = ROWS + half * HALF
    return jnp.concatenate(
        [ref[at : at + DEPTH, :], ref[at + DEPTH : at + 2 * DEPTH, :]], axis=1
    )


def docs(ref, half):
    rows = ref[2 * ROWS : 2 * ROWS + 16, :].astype(F32)
    return jnp.concatenate(
        [rows[2 * half : 2 * half + 1, :], rows[2 * half + 1 : 2 * half + 2, :]], axis=1
    )


def column(row):
    return jnp.broadcast_to(row, (DEPTH, row.shape[1])).T


def widen(col, lanes):
    return jnp.concatenate([col] * (lanes // DEPTH), axis=1)


def first_doc(own_ref):
    return docs(own_ref, 0)[:, 0:1]


def row_mask(own_ref):
    both = jnp.concatenate([docs(own_ref, 0), docs(own_ref, 1)], axis=1)
    return jnp.where(both == first_doc(own_ref), 1.0, 0.0)


def row_bias(own_ref):
    return (1.0 - row_mask(own_ref)) * NEG


def key_match(own_ref, ref, half):
    return jnp.where(docs(ref, half) == first_doc(own_ref), 1.0, 0.0)


def key_bias(own_ref, ref, half):
    return column((1.0 - key_match(own_ref, ref, half)) * NEG)


def dot(a, b):
    return jnp.dot(a, b, preferred_element_type=F32)


def fold(e):
    return jnp.sum(e.reshape(e.shape[0] // 8, 8, e.shape[1]), axis=0)


def all_keys(ref):
    return ref[0:ROWS, :]


def all_values(ref):
    return jnp.concatenate([values(ref, 0), values(ref, 1)], axis=1)


def head(h):
    return slice(h * DEPTH, (h + 1) * DEPTH)


def eight(h):
    return slice(h * 8, (h + 1) * 8)


def staged(units, first, rest, depth=1):
    held = [first(u) for u in units[:depth]]
    for i, u in enumerate(units):
        if i + depth < len(units):
            held.append(first(units[i + depth]))
        rest(u, held.pop(0))


def triangle(strict):
    key = lax.broadcasted_iota(jnp.int32, (HALF, HALF), 0)
    row = lax.broadcasted_iota(jnp.int32, (HALF, HALF), 1)
    keep = key > row if strict else key <= row
    return jnp.where(keep, 0.0, NEG)


def beside_keys(own_ref, ref):
    both = jnp.concatenate([key_match(own_ref, ref, k) for k in range(2)], axis=1)
    at = lax.broadcasted_iota(jnp.int32, (DEPTH, ROWS), 0)
    rows = jnp.where(at < 64, (1.0 - both) * NEG, 1.0)
    return rows.astype(BF16).T


def below_queries(own_ref):
    at = lax.broadcasted_iota(jnp.int32, (DEPTH, ROWS), 0)
    row = jnp.where(at == 64, row_bias(own_ref), 0.0)
    return jnp.where(at == 0, 1.0, row).astype(BF16)


def full_heads(own_ref, ref, qt_ref, acc_in, sum_in, put, depth):
    kk = jnp.concatenate([all_keys(ref), beside_keys(own_ref, ref)], axis=1)
    vv = all_values(ref)
    below = below_queries(own_ref)

    def first(h):
        return dot(kk, jnp.concatenate([qt_ref[head(h), :], below], axis=0))

    def rest(h, s):
        e = jnp.exp2(s * SCALE)
        o = dot(vv, e.astype(BF16))
        put(h, acc_in[head(h), :] + o, sum_in[eight(h), :] + fold(e))

    staged(range(HEADS), first, rest, depth)


def cut_heads(qt_ref, b_ref, kk, vv, cut, put):
    def first(u):
        h, r = u
        return dot(kk[r], qt_ref[head(h), r * HALF : (r + 1) * HALF])

    def rest(u, s):
        h, r = u
        e = jnp.exp2(s * SCALE + b_ref[cut[r], :])
        put(h, slice(r * HALF, (r + 1) * HALF), dot(vv[r], e.astype(BF16)), fold(e))

    staged([(h, r) for h in range(HEADS) for r in range(2)], first, rest, 2)


def own_block(q_ref, own_ref, qt_ref, acc_ref, sum_ref, b_ref, q_s, sem):
    copies = [
        pltpu.make_async_copy(q_ref.at[:, head(h)], q_s.at[:, head(h)], sem.at[h])
        for h in range(HEADS)
    ]
    for c in copies:
        c.start()
    rows = [docs(own_ref, 0), docs(own_ref, 1)]
    cols = [widen(column(r), HALF) for r in rows]
    apart = lambda k, r: jnp.where(cols[k] == rows[r], 0.0, NEG)
    tri = triangle(False)
    b_ref[0:HALF, :] = apart(0, 1)
    b_ref[HALF:ROWS, :] = apart(1, 1) + tri
    b_ref[ROWS : ROWS + HALF, :] = apart(0, 0) + tri
    for h in range(HEADS):
        copies[h].wait()
        qt_ref[head(h), :] = q_s[:, head(h)].T

    def put(h, cs, o, t):
        acc_ref[head(h), cs] = o
        sum_ref[eight(h), cs] = t

    cut_heads(
        qt_ref,
        b_ref,
        (keys(own_ref, 0), all_keys(own_ref)),
        (values(own_ref, 0), all_values(own_ref)),
        (slice(ROWS, ROWS + HALF), slice(0, ROWS)),
        put,
    )


def full_block(own_ref, ref, qt_ref, acc_in, sum_in, acc_ref, sum_ref):
    def put(h, acc, sums):
        acc_ref[head(h), :] = acc
        sum_ref[eight(h), :] = sums

    full_heads(own_ref, ref, qt_ref, acc_in, sum_in, put, 1)


def far_heads(own_ref, ref, qt_ref, acc_in, sum_in, tri_ref, put):
    left, right = slice(0, HALF), slice(HALF, ROWS)
    tri_ref[...] = triangle(True)
    beside = beside_keys(own_ref, ref)
    k0 = jnp.concatenate([keys(ref, 0), beside[left, :]], axis=1)
    k1 = jnp.concatenate([keys(ref, 1), beside[right, :]], axis=1)
    below = below_queries(own_ref)
    both = lambda a, b: jnp.concatenate([a, b], axis=1)

    def first(h):
        q = jnp.concatenate([qt_ref[head(h), :], below], axis=0)
        return dot(k0, q[:, left]), dot(k1, q)

    def rest(h, s):
        s0, s1 = s
        tri = tri_ref[...]
        e0 = jnp.exp2(s0 * SCALE + tri)
        e1 = jnp.exp2(both(s1[:, left] * SCALE, s1[:, right] * SCALE + tri))
        o1, t1 = dot(values(ref, 1), e1.astype(BF16)), fold(e1)
        o0 = dot(values(ref, 0), e0.astype(BF16)) + o1[:, left]
        t0 = fold(e0) + t1[:, left]
        acc = acc_in[head(h), :] + both(o0, o1[:, right])
        put(h, acc, sum_in[eight(h), :] + both(t0, t1[:, right]))

    staged(range(HEADS), first, rest, 2)


def careful(own_ref, full_refs, far_ref, qt_ref, out_ref, s_ref):
    refs = (own_ref, *full_refs, far_ref)
    lanes = 128
    key0 = lax.broadcasted_iota(jnp.int32, (HALF, lanes), 0)
    row0 = lax.broadcasted_iota(jnp.int32, (HALF, lanes), 1)
    mask = row_mask(own_ref)

    def one(step, carry):
        h, c = step // 4, step % 4
        hs = pl.ds(pl.multiple_of(h * DEPTH, DEPTH), DEPTH)
        cs = pl.ds(pl.multiple_of(c * lanes, lanes), lanes)
        qt = qt_ref[hs, cs]
        row = row0 + c * lanes
        both = [docs(own_ref, r // 2)[:, r % 2 * 128 : r % 2 * 128 + 128] for r in range(4)]
        own_row = mrow = None
        for r in range(4):
            picked = jnp.where(c == r, both[r], 0.0)
            m = jnp.where(c == r, mask[:, r * 128 : (r + 1) * 128], 0.0)
            own_row = picked if own_row is None else own_row + picked
            mrow = m if mrow is None else mrow + m
        for n, ref in enumerate(refs):
            for k in range(2):
                key = key0 + k * HALF
                col = column(docs(ref, k))
                if n == 0:
                    keep = (col == own_row) & (key <= row)
                else:
                    keep = (column(key_match(own_ref, ref, k)) * mrow) > 0.5
                    if ref is far_ref:
                        keep = keep & (key > row)
                s = dot(keys(ref, k), qt) * SCALE
                at = (2 * n + k) * HALF
                s_ref[at : at + HALF, :] = jnp.where(keep, s, NEG)
        top = jnp.max(s_ref[...], axis=0, keepdims=True)
        o, t = jnp.zeros((DEPTH, lanes), F32), jnp.zeros((1, lanes), F32)
        for n, ref in enumerate(refs):
            for k in range(2):
                at = (2 * n + k) * HALF
                e = jnp.exp2(s_ref[at : at + HALF, :] - top)
                t = t + jnp.sum(e, axis=0, keepdims=True)
                o = o + dot(values(ref, k), e.astype(BF16))
        out_ref[cs, hs] = (o / t).T.astype(BF16)
        return carry

    lax.fori_loop(0, HEADS * 4, one, 0)


def last_block(
    own_ref, pa_ref, e1_ref, e2_ref, far_ref, qt_ref, acc_in, sum_in,
    out_ref, o_s, s_ref, good_ref, tri_ref, sem,
):
    copies = [
        pltpu.make_async_copy(o_s.at[rows, :], out_ref.at[rows, :], sem.at[n])
        for n, rows in enumerate(slice(a, a + 128) for a in range(0, ROWS, 128))
    ]

    def put(h, acc, sums):
        t = jnp.sum(sums, axis=0, keepdims=True)
        good_ref[h : h + 1, :] = jnp.where((t > LOW) & (t < HIGH), 1.0, 0.0)
        o_s[:, head(h)] = (acc * (1.0 / t)).astype(BF16).T

    far_heads(own_ref, far_ref, qt_ref, acc_in, sum_in, tri_ref, put)
    for c in copies:
        c.start()
    bad = jnp.min(good_ref[...]) < 0.5
    for c in copies:
        c.wait()

    @pl.when(bad)
    def _():
        careful(own_ref, (pa_ref, e1_ref, e2_ref), far_ref, qt_ref, o_s, s_ref)
        for c in copies:
            c.start()
        for c in copies:
            c.wait()


def local(queries, k, v, doc_ids):
    size = lax.axis_size("ctx")
    block = jax.ShapeDtypeStruct(BLOCK, BF16)
    qt_out = jax.ShapeDtypeStruct(QT, BF16)
    acc_out = jax.ShapeDtypeStruct(QT, F32)
    sum_out = jax.ShapeDtypeStruct(SUMS, F32)
    dma = pltpu.SemaphoreType.DMA

    def move(x, pairs):
        return lax.ppermute(x, "ctx", [(a, b) for a, b in pairs if 0 <= b < size])

    own = call(
        pack,
        jax.ShapeDtypeStruct(SENT, BF16),
        (ANY, ANY, ANY),
        scratch=(
            pltpu.VMEM((ROWS, DEPTH), BF16),
            pltpu.VMEM((1, ROWS), jnp.int32),
            dma((3,)),
        ),
    )(in_hbm(k), in_hbm(v), in_hbm(doc_ids))
    px = move(own, [(i, i + 4) for i in range(1, size, 2)])
    pa = move(own, [(i, i + (1 if i % 2 else 3)) for i in range(size)])
    py = move(own, [(i, i + 4) for i in range(0, size, 2)])
    qt, acc, sums = call(
        own_block,
        (qt_out, acc_out, sum_out),
        (ANY, VM),
        scratch=(BIAS, pltpu.VMEM((ROWS, HEADS * DEPTH), BF16), dma((HEADS,))),
    )(in_hbm(queries), own)
    swap = [(i, i ^ 1) for i in range(size)]
    hand_over = call(hand, block, (VM, VM, ANY))
    full = call(full_block, (acc_out, sum_out))
    e1 = move(hand_over(own, px, sums), swap)
    acc, sums = full(own, e1, qt, acc, sums)
    e2 = move(hand_over(pa, pa, sums), swap)
    acc, sums = full(own, pa, qt, acc, sums)
    acc, sums = full(own, e2, qt, acc, sums)
    far = hand_over(py, px, sums)
    return call(
        last_block,
        jax.ShapeDtypeStruct(queries.shape, BF16),
        outs=ANY,
        scratch=(
            pltpu.VMEM((ROWS, HEADS * DEPTH), BF16),
            pltpu.VMEM((10 * HALF, 128), F32),
            pltpu.VMEM((HEADS, ROWS), F32),
            TRI,
            dma((4,)),
        ),
    )(own, pa, e1, e2, far, qt, acc, sums)


def solution(mesh):
    return jax.shard_map(
        local,
        mesh=mesh,
        in_specs=(P("ctx", None), P("ctx", None), P("ctx", None), P("ctx")),
        out_specs=P("ctx", None),
        check_vma=False,
    )
```

```python
import jax
import jax.numpy as jnp
from jax import lax
from jax.experimental import pallas as pl
from jax.experimental.pallas import tpu as pltpu
from jax.sharding import PartitionSpec as P

ROWS = 512
HALF = 256
DEPTH = 128
HEADS = 8
SCALE = 1.4426950408889634 / DEPTH**0.5
NEG = -1e30
LOW, HIGH = 2.0**-60, 2.0**100
VM = pl.BlockSpec(memory_space=pltpu.VMEM)
SENT = (2 * ROWS + 32, DEPTH)
BLOCK = (2 * ROWS + 16, DEPTH)
QT = (HEADS * DEPTH, ROWS)
SUMS = (HEADS * 8, ROWS)
F32 = jnp.float32
BF16 = jnp.bfloat16


ANY = pl.BlockSpec(memory_space=pl.ANY)
BIAS = pltpu.VMEM((ROWS + HALF, HALF), F32)
TRI = pltpu.VMEM((HALF, HALF), F32)


def call(body, out, ins=None, outs=None, scratch=()):
    return pl.pallas_call(
        body,
        out_shape=out,
        **({} if ins is None else {"in_specs": ins}),
        out_specs=outs or jax.tree.map(lambda _: VM, out),
        scratch_shapes=scratch,
        cost_estimate=pl.CostEstimate(flops=1, bytes_accessed=1, transcendentals=0),
        compiler_params=pltpu.CompilerParams(vmem_limit_bytes=16 << 20),
    )


def in_hbm(x):
    return pltpu.with_memory_space_constraint(x, pltpu.HBM)


def pack(k_ref, v_ref, d_ref, o_ref, v_s, d_s, sem):
    copies = [
        pltpu.make_async_copy(v_ref, v_s, sem.at[0]),
        pltpu.make_async_copy(d_ref, d_s.at[0], sem.at[1]),
        pltpu.make_async_copy(k_ref, o_ref.at[0:ROWS, :], sem.at[2]),
    ]
    for c in copies:
        c.start()
    copies[1].wait()
    d = (d_s[...] + 1).astype(F32)
    rows = [d[:, a : a + DEPTH] for a in range(0, ROWS, DEPTH)]
    pad = jnp.zeros((SENT[0] - 2 * ROWS - 4, DEPTH), F32)
    o_ref[2 * ROWS :, :] = jnp.concatenate([*rows, pad], axis=0).astype(BF16)
    copies[0].wait()
    for a in range(0, ROWS, DEPTH):
        o_ref[ROWS + a : ROWS + a + DEPTH, :] = v_s[a : a + DEPTH, :].T
    copies[2].wait()


def hand(even_ref, odd_ref, after_ref, also_ref, o_ref):
    core = lax.axis_index("ctx") % 2

    @pl.when(core == 0)
    def _():
        o_ref[...] = even_ref[0 : BLOCK[0], :]

    @pl.when(core == 1)
    def _():
        o_ref[...] = odd_ref[0 : BLOCK[0], :]


def keys(ref, half):
    return ref[half * HALF : (half + 1) * HALF, :]


def values(ref, half):
    at = ROWS + half * HALF
    return jnp.concatenate(
        [ref[at : at + DEPTH, :], ref[at + DEPTH : at + 2 * DEPTH, :]], axis=1
    )


def docs(ref, half):
    rows = ref[2 * ROWS : 2 * ROWS + 16, :].astype(F32)
    return jnp.concatenate(
        [rows[2 * half : 2 * half + 1, :], rows[2 * half + 1 : 2 * half + 2, :]], axis=1
    )


def column(row):
    return jnp.broadcast_to(row, (DEPTH, row.shape[1])).T


def widen(col, lanes):
    return jnp.concatenate([col] * (lanes // DEPTH), axis=1)


def first_doc(own_ref):
    return docs(own_ref, 0)[:, 0:1]


def row_mask(own_ref):
    both = jnp.concatenate([docs(own_ref, 0), docs(own_ref, 1)], axis=1)
    return jnp.where(both == first_doc(own_ref), 1.0, 0.0)


def row_bias(own_ref):
    return (1.0 - row_mask(own_ref)) * NEG


def key_match(own_ref, ref, half):
    return jnp.where(docs(ref, half) == first_doc(own_ref), 1.0, 0.0)


def key_bias(own_ref, ref, half):
    return column((1.0 - key_match(own_ref, ref, half)) * NEG)


def dot(a, b):
    return jnp.dot(a, b, preferred_element_type=F32)


def fold(e):
    return jnp.sum(e.reshape(e.shape[0] // 8, 8, e.shape[1]), axis=0)


def all_keys(ref):
    return ref[0:ROWS, :]


def all_values(ref):
    return jnp.concatenate([values(ref, 0), values(ref, 1)], axis=1)


def head(h):
    return slice(h * DEPTH, (h + 1) * DEPTH)


def eight(h):
    return slice(h * 8, (h + 1) * 8)


def staged(units, first, rest, depth=1):
    held = [first(u) for u in units[:depth]]
    for i, u in enumerate(units):
        if i + depth < len(units):
            held.append(first(units[i + depth]))
        rest(u, held.pop(0))


def triangle(strict):
    key = lax.broadcasted_iota(jnp.int32, (HALF, HALF), 0)
    row = lax.broadcasted_iota(jnp.int32, (HALF, HALF), 1)
    keep = key > row if strict else key <= row
    return jnp.where(keep, 0.0, NEG)


def beside_keys(own_ref, ref):
    both = jnp.concatenate([key_match(own_ref, ref, k) for k in range(2)], axis=1)
    at = lax.broadcasted_iota(jnp.int32, (DEPTH, ROWS), 0)
    rows = jnp.where(at < 64, (1.0 - both) * NEG, 1.0)
    return rows.astype(BF16).T


def below_queries(own_ref):
    at = lax.broadcasted_iota(jnp.int32, (DEPTH, ROWS), 0)
    row = jnp.where(at == 64, row_bias(own_ref), 0.0)
    return jnp.where(at == 0, 1.0, row).astype(BF16)


def full_heads(own_ref, ref, qt_ref, acc_in, sum_in, put, depth):
    kk = jnp.concatenate([all_keys(ref), beside_keys(own_ref, ref)], axis=1)
    vv = all_values(ref)
    below = below_queries(own_ref)

    def first(h):
        return dot(kk, jnp.concatenate([qt_ref[head(h), :], below], axis=0))

    def rest(h, s):
        e = jnp.exp2(s * SCALE)
        o = dot(vv, e.astype(BF16))
        put(h, acc_in[head(h), :] + o, sum_in[eight(h), :] + fold(e))

    staged(range(HEADS), first, rest, depth)


def cut_heads(qt_ref, b_ref, kk, vv, cut, put):
    def first(u):
        h, r = u
        return dot(kk[r], qt_ref[head(h), r * HALF : (r + 1) * HALF])

    def rest(u, s):
        h, r = u
        e = jnp.exp2(s * SCALE + b_ref[cut[r], :])
        put(h, slice(r * HALF, (r + 1) * HALF), dot(vv[r], e.astype(BF16)), fold(e))

    staged([(h, r) for h in range(HEADS) for r in range(2)], first, rest, 2)


def own_block(q_ref, own_ref, qt_ref, acc_ref, sum_ref, b_ref, q_s, sem):
    copies = [
        pltpu.make_async_copy(q_ref.at[:, head(h)], q_s.at[:, head(h)], sem.at[h])
        for h in range(HEADS)
    ]
    for c in copies:
        c.start()
    rows = [docs(own_ref, 0), docs(own_ref, 1)]
    cols = [widen(column(r), HALF) for r in rows]
    apart = lambda k, r: jnp.where(cols[k] == rows[r], 0.0, NEG)
    tri = triangle(False)
    b_ref[0:HALF, :] = apart(0, 1)
    b_ref[HALF:ROWS, :] = apart(1, 1) + tri
    b_ref[ROWS : ROWS + HALF, :] = apart(0, 0) + tri
    for h in range(HEADS):
        copies[h].wait()
        qt_ref[head(h), :] = q_s[:, head(h)].T

    def put(h, cs, o, t):
        acc_ref[head(h), cs] = o
        sum_ref[eight(h), cs] = t

    cut_heads(
        qt_ref,
        b_ref,
        (keys(own_ref, 0), all_keys(own_ref)),
        (values(own_ref, 0), all_values(own_ref)),
        (slice(ROWS, ROWS + HALF), slice(0, ROWS)),
        put,
    )


def full_block(own_ref, ref, qt_ref, acc_in, sum_in, acc_ref, sum_ref):
    def put(h, acc, sums):
        acc_ref[head(h), :] = acc
        sum_ref[eight(h), :] = sums

    full_heads(own_ref, ref, qt_ref, acc_in, sum_in, put, 1)


def far_block(own_ref, ref, qt_ref, acc_in, sum_in, acc_ref, sum_ref, b_ref):
    left, right = slice(0, HALF), slice(HALF, ROWS)

    b_ref[...] = triangle(True)
    beside = beside_keys(own_ref, ref)
    k0 = jnp.concatenate([keys(ref, 0), beside[left, :]], axis=1)
    k1 = jnp.concatenate([keys(ref, 1), beside[right, :]], axis=1)
    below = below_queries(own_ref)

    def first(h):
        q = jnp.concatenate([qt_ref[head(h), :], below], axis=0)
        return dot(k0, q[:, left]), dot(k1, q)

    def rest(h, s):
        s0, s1 = s
        tri = b_ref[...]
        e0 = jnp.exp2(s0 * SCALE + tri)
        cut = jnp.concatenate([s1[:, left] * SCALE, s1[:, right] * SCALE + tri], axis=1)
        e1 = jnp.exp2(cut)
        o1, t1 = dot(values(ref, 1), e1.astype(BF16)), fold(e1)
        o0 = dot(values(ref, 0), e0.astype(BF16)) + o1[:, left]
        t0 = fold(e0) + t1[:, left]
        acc_ref[head(h), left] = acc_in[head(h), left] + o0
        acc_ref[head(h), right] = acc_in[head(h), right] + o1[:, right]
        sum_ref[eight(h), left] = sum_in[eight(h), left] + t0
        sum_ref[eight(h), right] = sum_in[eight(h), right] + t1[:, right]

    staged(range(HEADS), first, rest, 2)


def careful(own_ref, full_refs, far_ref, qt_ref, out_ref, s_ref):
    refs = (own_ref, *full_refs, far_ref)
    lanes = 128
    key0 = lax.broadcasted_iota(jnp.int32, (HALF, lanes), 0)
    row0 = lax.broadcasted_iota(jnp.int32, (HALF, lanes), 1)
    mask = row_mask(own_ref)

    def one(step, carry):
        h, c = step // 4, step % 4
        hs = pl.ds(pl.multiple_of(h * DEPTH, DEPTH), DEPTH)
        cs = pl.ds(pl.multiple_of(c * lanes, lanes), lanes)
        qt = qt_ref[hs, cs]
        row = row0 + c * lanes
        both = [docs(own_ref, r // 2)[:, r % 2 * 128 : r % 2 * 128 + 128] for r in range(4)]
        own_row = mrow = None
        for r in range(4):
            picked = jnp.where(c == r, both[r], 0.0)
            m = jnp.where(c == r, mask[:, r * 128 : (r + 1) * 128], 0.0)
            own_row = picked if own_row is None else own_row + picked
            mrow = m if mrow is None else mrow + m
        for n, ref in enumerate(refs):
            for k in range(2):
                key = key0 + k * HALF
                col = column(docs(ref, k))
                if n == 0:
                    keep = (col == own_row) & (key <= row)
                else:
                    keep = (column(key_match(own_ref, ref, k)) * mrow) > 0.5
                    if ref is far_ref:
                        keep = keep & (key > row)
                s = dot(keys(ref, k), qt) * SCALE
                at = (2 * n + k) * HALF
                s_ref[at : at + HALF, :] = jnp.where(keep, s, NEG)
        top = jnp.max(s_ref[...], axis=0, keepdims=True)
        o, t = jnp.zeros((DEPTH, lanes), F32), jnp.zeros((1, lanes), F32)
        for n, ref in enumerate(refs):
            for k in range(2):
                at = (2 * n + k) * HALF
                e = jnp.exp2(s_ref[at : at + HALF, :] - top)
                t = t + jnp.sum(e, axis=0, keepdims=True)
                o = o + dot(values(ref, k), e.astype(BF16))
        out_ref[cs, hs] = (o / t).T.astype(BF16)
        return carry

    lax.fori_loop(0, HEADS * 4, one, 0)


def last_block(
    own_ref, pa_ref, pb_ref, e1_ref, e2_ref, qt_ref, acc_in, sum_in,
    out_ref, o_s, s_ref, good_ref, sem,
):
    copies = [
        pltpu.make_async_copy(o_s.at[rows, :], out_ref.at[rows, :], sem.at[n])
        for n, rows in enumerate(slice(a, a + 128) for a in range(0, ROWS, 128))
    ]

    def put(h, acc, sums):
        t = jnp.sum(sums, axis=0, keepdims=True)
        good_ref[h : h + 1, :] = jnp.where((t > LOW) & (t < HIGH), 1.0, 0.0)
        o_s[:, head(h)] = (acc * (1.0 / t)).astype(BF16).T

    full_heads(own_ref, e2_ref, qt_ref, acc_in, sum_in, put, 2)
    for c in copies:
        c.start()
    bad = jnp.min(good_ref[...]) < 0.5
    for c in copies:
        c.wait()

    @pl.when(bad)
    def _():
        careful(own_ref, (pa_ref, e1_ref, e2_ref), pb_ref, qt_ref, o_s, s_ref)
        for c in copies:
            c.start()
        for c in copies:
            c.wait()


def local(queries, k, v, doc_ids):
    size = lax.axis_size("ctx")
    block = jax.ShapeDtypeStruct(BLOCK, BF16)
    qt_out = jax.ShapeDtypeStruct(QT, BF16)
    acc_out = jax.ShapeDtypeStruct(QT, F32)
    sum_out = jax.ShapeDtypeStruct(SUMS, F32)
    dma = pltpu.SemaphoreType.DMA

    def move(x, pairs):
        return lax.ppermute(x, "ctx", [(a, b) for a, b in pairs if 0 <= b < size])

    own = call(
        pack,
        jax.ShapeDtypeStruct(SENT, BF16),
        (ANY, ANY, ANY),
        scratch=(
            pltpu.VMEM((ROWS, DEPTH), BF16),
            pltpu.VMEM((1, ROWS), jnp.int32),
            dma((3,)),
        ),
    )(in_hbm(k), in_hbm(v), in_hbm(doc_ids))
    px = move(own, [(i, i + 4) for i in range(1, size, 2)])
    pa = move(own, [(i, i + (1 if i % 2 else 3)) for i in range(size)])
    py = move(own, [(i, i + 4) for i in range(0, size, 2)])
    qt, acc, sums = call(
        own_block,
        (qt_out, acc_out, sum_out),
        (ANY, VM),
        scratch=(BIAS, pltpu.VMEM((ROWS, HEADS * DEPTH), BF16), dma((HEADS,))),
    )(in_hbm(queries), own)
    swap = [(i, i ^ 1) for i in range(size)]
    hand_over = call(hand, block, (VM, VM, ANY, ANY))
    full = call(full_block, (acc_out, sum_out))
    e1 = move(hand_over(own, px, sums, sums), swap)
    acc, sums = full(own, e1, qt, acc, sums)
    acc, sums = full(own, pa, qt, acc, sums)
    e2 = move(hand_over(pa, pa, sums, py), swap)
    far = hand_over(py, px, sums, sums)
    acc, sums = call(far_block, (acc_out, sum_out), scratch=(TRI,))(
        own, far, qt, acc, sums
    )
    return call(
        last_block,
        jax.ShapeDtypeStruct(queries.shape, BF16),
        outs=ANY,
        scratch=(
            pltpu.VMEM((ROWS, HEADS * DEPTH), BF16),
            pltpu.VMEM((10 * HALF, 128), F32),
            pltpu.VMEM((HEADS, ROWS), F32),
            dma((4,)),
        ),
    )(own, pa, far, e1, e2, qt, acc, sums)


def solution(mesh):
    return jax.shard_map(
        local,
        mesh=mesh,
        in_specs=(P("ctx", None), P("ctx", None), P("ctx", None), P("ctx")),
        out_specs=P("ctx", None),
        check_vma=False,
    )
```

```python
import jax
import jax.numpy as jnp
from jax import lax
from jax.experimental import pallas as pl
from jax.experimental.pallas import tpu as pltpu
from jax.sharding import PartitionSpec as P

ROWS = 512
HALF = 256
DEPTH = 128
HEADS = 8
SCALE = 1.4426950408889634 / DEPTH**0.5
NEG = -1e30
LOW, HIGH = 2.0**-60, 2.0**100
VM = pl.BlockSpec(memory_space=pltpu.VMEM)
SENT = (2 * ROWS + 32, DEPTH)
BLOCK = (2 * ROWS + 16, DEPTH)
QT = (HEADS * DEPTH, ROWS)
SUMS = (HEADS * 8, ROWS)
F32 = jnp.float32
BF16 = jnp.bfloat16


ANY = pl.BlockSpec(memory_space=pl.ANY)
BIAS = pltpu.VMEM((ROWS + HALF, HALF), F32)
TRI = pltpu.VMEM((HALF, HALF), F32)


def call(body, out, ins=None, outs=None, scratch=()):
    return pl.pallas_call(
        body,
        out_shape=out,
        **({} if ins is None else {"in_specs": ins}),
        out_specs=outs or jax.tree.map(lambda _: VM, out),
        scratch_shapes=scratch,
        cost_estimate=pl.CostEstimate(flops=1, bytes_accessed=1, transcendentals=0),
        compiler_params=pltpu.CompilerParams(vmem_limit_bytes=16 << 20),
    )


def in_hbm(x):
    return pltpu.with_memory_space_constraint(x, pltpu.HBM)


def pack(k_ref, v_ref, d_ref, o_ref, v_s, d_s, sem):
    parts = [slice(a, a + DEPTH) for a in range(0, ROWS, DEPTH)]
    docs_in = pltpu.make_async_copy(d_ref, d_s.at[0], sem.at[0])
    values_in = [
        pltpu.make_async_copy(v_ref.at[p, :], v_s.at[p, :], sem.at[1 + n])
        for n, p in enumerate(parts)
    ]
    keys_in = [
        pltpu.make_async_copy(k_ref.at[p, :], o_ref.at[p, :], sem.at[5 + n])
        for n, p in enumerate(parts)
    ]
    for c in (*values_in, docs_in, *keys_in):
        c.start()
    docs_in.wait()
    d = (d_s[...] + 1).astype(F32)
    rows = [d[:, a : a + DEPTH] for a in range(0, ROWS, DEPTH)]
    pad = jnp.zeros((SENT[0] - 2 * ROWS - 4, DEPTH), F32)
    o_ref[2 * ROWS :, :] = jnp.concatenate([*rows, pad], axis=0).astype(BF16)
    for c in values_in:
        c.wait()
    for a in range(0, ROWS, DEPTH):
        o_ref[ROWS + a : ROWS + a + DEPTH, :] = v_s[a : a + DEPTH, :].T
    for c in keys_in:
        c.wait()


def hand(even_ref, odd_ref, after_ref, o_ref):
    core = lax.axis_index("ctx") % 2

    @pl.when(core == 0)
    def _():
        o_ref[...] = even_ref[0 : BLOCK[0], :]

    @pl.when(core == 1)
    def _():
        o_ref[...] = odd_ref[0 : BLOCK[0], :]


def keys(ref, half):
    return ref[half * HALF : (half + 1) * HALF, :]


def values(ref, half):
    at = ROWS + half * HALF
    return jnp.concatenate(
        [ref[at : at + DEPTH, :], ref[at + DEPTH : at + 2 * DEPTH, :]], axis=1
    )


def docs(ref, half):
    rows = ref[2 * ROWS : 2 * ROWS + 16, :].astype(F32)
    return jnp.concatenate(
        [rows[2 * half : 2 * half + 1, :], rows[2 * half + 1 : 2 * half + 2, :]], axis=1
    )


def column(row):
    return jnp.broadcast_to(row, (DEPTH, row.shape[1])).T


def widen(col, lanes):
    return jnp.concatenate([col] * (lanes // DEPTH), axis=1)


def first_doc(own_ref):
    return docs(own_ref, 0)[:, 0:1]


def row_mask(own_ref):
    both = jnp.concatenate([docs(own_ref, 0), docs(own_ref, 1)], axis=1)
    return jnp.where(both == first_doc(own_ref), 1.0, 0.0)


def row_bias(own_ref):
    return (1.0 - row_mask(own_ref)) * NEG


def key_match(own_ref, ref, half):
    return jnp.where(docs(ref, half) == first_doc(own_ref), 1.0, 0.0)


def key_bias(own_ref, ref, half):
    return column((1.0 - key_match(own_ref, ref, half)) * NEG)


def dot(a, b):
    return jnp.dot(a, b, preferred_element_type=F32)


def fold(e):
    return jnp.sum(e.reshape(e.shape[0] // 8, 8, e.shape[1]), axis=0)


def all_keys(ref):
    return ref[0:ROWS, :]


def all_values(ref):
    return jnp.concatenate([values(ref, 0), values(ref, 1)], axis=1)


def head(h):
    return slice(h * DEPTH, (h + 1) * DEPTH)


def eight(h):
    return slice(h * 8, (h + 1) * 8)


def staged(units, first, rest, depth=1):
    held = [first(u) for u in units[:depth]]
    for i, u in enumerate(units):
        if i + depth < len(units):
            held.append(first(units[i + depth]))
        rest(u, held.pop(0))


def triangle(strict):
    key = lax.broadcasted_iota(jnp.int32, (HALF, HALF), 0)
    row = lax.broadcasted_iota(jnp.int32, (HALF, HALF), 1)
    keep = key > row if strict else key <= row
    return jnp.where(keep, 0.0, NEG)


def beside_keys(own_ref, ref):
    both = jnp.concatenate([key_match(own_ref, ref, k) for k in range(2)], axis=1)
    at = lax.broadcasted_iota(jnp.int32, (DEPTH, ROWS), 0)
    rows = jnp.where(at < 64, (1.0 - both) * NEG, 1.0)
    return rows.astype(BF16).T


def below_queries(own_ref):
    at = lax.broadcasted_iota(jnp.int32, (DEPTH, ROWS), 0)
    row = jnp.where(at == 64, row_bias(own_ref), 0.0)
    return jnp.where(at == 0, 1.0, row).astype(BF16)


def full_heads(own_ref, ref, qt_ref, acc_in, sum_in, put, depth):
    kk = jnp.concatenate([all_keys(ref), beside_keys(own_ref, ref)], axis=1)
    vv = all_values(ref)
    below = below_queries(own_ref)

    def first(h):
        return dot(kk, jnp.concatenate([qt_ref[head(h), :], below], axis=0))

    def rest(h, s):
        e = jnp.exp2(s * SCALE)
        o = dot(vv, e.astype(BF16))
        put(h, acc_in[head(h), :] + o, sum_in[eight(h), :] + fold(e))

    staged(range(HEADS), first, rest, depth)


def cut_heads(qt_ref, b_ref, kk, vv, cut, put):
    def first(u):
        h, r = u
        return dot(kk[r], qt_ref[head(h), r * HALF : (r + 1) * HALF])

    def rest(u, s):
        h, r = u
        e = jnp.exp2(s * SCALE + b_ref[cut[r], :])
        put(h, slice(r * HALF, (r + 1) * HALF), dot(vv[r], e.astype(BF16)), fold(e))

    staged([(h, r) for h in range(HEADS) for r in range(2)], first, rest, 2)


def own_block(q_ref, own_ref, qt_ref, acc_ref, sum_ref, b_ref, q_s, sem):
    copies = [
        pltpu.make_async_copy(q_ref.at[:, head(h)], q_s.at[:, head(h)], sem.at[h])
        for h in range(HEADS)
    ]
    for c in copies:
        c.start()
    rows = [docs(own_ref, 0), docs(own_ref, 1)]
    cols = [widen(column(r), HALF) for r in rows]
    apart = lambda k, r: jnp.where(cols[k] == rows[r], 0.0, NEG)
    tri = triangle(False)
    b_ref[0:HALF, :] = apart(0, 1)
    b_ref[HALF:ROWS, :] = apart(1, 1) + tri
    b_ref[ROWS : ROWS + HALF, :] = apart(0, 0) + tri
    for h in range(HEADS):
        copies[h].wait()
        qt_ref[head(h), :] = q_s[:, head(h)].T

    def put(h, cs, o, t):
        acc_ref[head(h), cs] = o
        sum_ref[eight(h), cs] = t

    cut_heads(
        qt_ref,
        b_ref,
        (keys(own_ref, 0), all_keys(own_ref)),
        (values(own_ref, 0), all_values(own_ref)),
        (slice(ROWS, ROWS + HALF), slice(0, ROWS)),
        put,
    )


def full_block(own_ref, ref, qt_ref, acc_in, sum_in, acc_ref, sum_ref):
    def put(h, acc, sums):
        acc_ref[head(h), :] = acc
        sum_ref[eight(h), :] = sums

    full_heads(own_ref, ref, qt_ref, acc_in, sum_in, put, 2)


def far_block(own_ref, ref, qt_ref, acc_in, sum_in, acc_ref, sum_ref, b_ref):
    left, right = slice(0, HALF), slice(HALF, ROWS)

    b_ref[...] = triangle(True)
    beside = beside_keys(own_ref, ref)
    k0 = jnp.concatenate([keys(ref, 0), beside[left, :]], axis=1)
    k1 = jnp.concatenate([keys(ref, 1), beside[right, :]], axis=1)
    below = below_queries(own_ref)

    def first(h):
        q = jnp.concatenate([qt_ref[head(h), :], below], axis=0)
        return dot(k0, q[:, left]), dot(k1, q)

    def rest(h, s):
        s0, s1 = s
        tri = b_ref[...]
        e0 = jnp.exp2(s0 * SCALE + tri)
        cut = jnp.concatenate([s1[:, left] * SCALE, s1[:, right] * SCALE + tri], axis=1)
        e1 = jnp.exp2(cut)
        o1, t1 = dot(values(ref, 1), e1.astype(BF16)), fold(e1)
        o0 = dot(values(ref, 0), e0.astype(BF16)) + o1[:, left]
        t0 = fold(e0) + t1[:, left]
        acc_ref[head(h), left] = acc_in[head(h), left] + o0
        acc_ref[head(h), right] = acc_in[head(h), right] + o1[:, right]
        sum_ref[eight(h), left] = sum_in[eight(h), left] + t0
        sum_ref[eight(h), right] = sum_in[eight(h), right] + t1[:, right]

    staged(range(HEADS), first, rest, 2)


def careful(own_ref, full_refs, far_ref, qt_ref, out_ref, s_ref):
    refs = (own_ref, *full_refs, far_ref)
    lanes = 128
    key0 = lax.broadcasted_iota(jnp.int32, (HALF, lanes), 0)
    row0 = lax.broadcasted_iota(jnp.int32, (HALF, lanes), 1)
    mask = row_mask(own_ref)

    def one(step, carry):
        h, c = step // 4, step % 4
        hs = pl.ds(pl.multiple_of(h * DEPTH, DEPTH), DEPTH)
        cs = pl.ds(pl.multiple_of(c * lanes, lanes), lanes)
        qt = qt_ref[hs, cs]
        row = row0 + c * lanes
        both = [docs(own_ref, r // 2)[:, r % 2 * 128 : r % 2 * 128 + 128] for r in range(4)]
        own_row = mrow = None
        for r in range(4):
            picked = jnp.where(c == r, both[r], 0.0)
            m = jnp.where(c == r, mask[:, r * 128 : (r + 1) * 128], 0.0)
            own_row = picked if own_row is None else own_row + picked
            mrow = m if mrow is None else mrow + m
        for n, ref in enumerate(refs):
            for k in range(2):
                key = key0 + k * HALF
                col = column(docs(ref, k))
                if n == 0:
                    keep = (col == own_row) & (key <= row)
                else:
                    keep = (column(key_match(own_ref, ref, k)) * mrow) > 0.5
                    if ref is far_ref:
                        keep = keep & (key > row)
                s = dot(keys(ref, k), qt) * SCALE
                at = (2 * n + k) * HALF
                s_ref[at : at + HALF, :] = jnp.where(keep, s, NEG)
        top = jnp.max(s_ref[...], axis=0, keepdims=True)
        o, t = jnp.zeros((DEPTH, lanes), F32), jnp.zeros((1, lanes), F32)
        for n, ref in enumerate(refs):
            for k in range(2):
                at = (2 * n + k) * HALF
                e = jnp.exp2(s_ref[at : at + HALF, :] - top)
                t = t + jnp.sum(e, axis=0, keepdims=True)
                o = o + dot(values(ref, k), e.astype(BF16))
        out_ref[cs, hs] = (o / t).T.astype(BF16)
        return carry

    lax.fori_loop(0, HEADS * 4, one, 0)


def last_block(
    own_ref, pa_ref, pb_ref, e1_ref, e2_ref, qt_ref, acc_in, sum_in,
    out_ref, o_s, s_ref, good_ref, sem,
):
    copies = [
        pltpu.make_async_copy(o_s.at[rows, :], out_ref.at[rows, :], sem.at[n])
        for n, rows in enumerate(slice(a, a + 128) for a in range(0, ROWS, 128))
    ]

    def put(h, acc, sums):
        t = jnp.sum(sums, axis=0, keepdims=True)
        good_ref[h : h + 1, :] = jnp.where((t > LOW) & (t < HIGH), 1.0, 0.0)
        o_s[:, head(h)] = (acc * (1.0 / t)).astype(BF16).T

    full_heads(own_ref, e2_ref, qt_ref, acc_in, sum_in, put, 2)
    for c in copies:
        c.start()
    bad = jnp.min(good_ref[...]) < 0.5
    for c in copies:
        c.wait()

    @pl.when(bad)
    def _():
        careful(own_ref, (pa_ref, e1_ref, e2_ref), pb_ref, qt_ref, o_s, s_ref)
        for c in copies:
            c.start()
        for c in copies:
            c.wait()


def local(queries, k, v, doc_ids):
    size = lax.axis_size("ctx")
    block = jax.ShapeDtypeStruct(BLOCK, BF16)
    qt_out = jax.ShapeDtypeStruct(QT, BF16)
    acc_out = jax.ShapeDtypeStruct(QT, F32)
    sum_out = jax.ShapeDtypeStruct(SUMS, F32)
    dma = pltpu.SemaphoreType.DMA

    def move(x, pairs):
        return lax.ppermute(x, "ctx", [(a, b) for a, b in pairs if 0 <= b < size])

    own = call(
        pack,
        jax.ShapeDtypeStruct(SENT, BF16),
        (ANY, ANY, ANY),
        scratch=(
            pltpu.VMEM((ROWS, DEPTH), BF16),
            pltpu.VMEM((1, ROWS), jnp.int32),
            dma((9,)),
        ),
    )(in_hbm(k), in_hbm(v), in_hbm(doc_ids))
    pa = move(own, [(i, i + (1 if i % 2 else 3)) for i in range(size)])
    pb = move(own, [(i, i + 4) for i in range(size)])
    qt, acc, sums = call(
        own_block,
        (qt_out, acc_out, sum_out),
        (ANY, VM),
        scratch=(BIAS, pltpu.VMEM((ROWS, HEADS * DEPTH), BF16), dma((HEADS,))),
    )(in_hbm(queries), own)
    swap = [(i, i ^ 1) for i in range(size)]
    hand_over = call(hand, block, (VM, VM, ANY))
    full = call(full_block, (acc_out, sum_out))
    e1 = move(hand_over(own, pb, sums), swap)
    acc, sums = call(far_block, (acc_out, sum_out), scratch=(TRI,))(
        own, pb, qt, acc, sums
    )
    acc, sums = full(own, e1, qt, acc, sums)
    e2 = move(hand_over(pa, pa, sums), swap)
    acc, sums = full(own, pa, qt, acc, sums)
    return call(
        last_block,
        jax.ShapeDtypeStruct(queries.shape, BF16),
        outs=ANY,
        scratch=(
            pltpu.VMEM((ROWS, HEADS * DEPTH), BF16),
            pltpu.VMEM((10 * HALF, 128), F32),
            pltpu.VMEM((HEADS, ROWS), F32),
            dma((4,)),
        ),
    )(own, pa, pb, e1, e2, qt, acc, sums)


def solution(mesh):
    return jax.shard_map(
        local,
        mesh=mesh,
        in_specs=(P("ctx", None), P("ctx", None), P("ctx", None), P("ctx")),
        out_specs=P("ctx", None),
        check_vma=False,
    )
```

```python
import jax
import jax.numpy as jnp
from jax import lax
from jax.experimental import pallas as pl
from jax.experimental.pallas import tpu as pltpu
from jax.sharding import PartitionSpec as P

ROWS = 512
HALF = 256
DEPTH = 128
HEADS = 8
SOLO = 5
SCALE = 1.4426950408889634 / DEPTH**0.5
NEG = -1e30
LOW, HIGH = 2.0**-60, 2.0**100
VM = pl.BlockSpec(memory_space=pltpu.VMEM)
SENT = (2 * ROWS + 32, DEPTH)
BLOCK = (2 * ROWS + 16, DEPTH)
QT = (HEADS * DEPTH, ROWS)
SUMS = (HEADS * 8, ROWS)
F32 = jnp.float32
BF16 = jnp.bfloat16


ANY = pl.BlockSpec(memory_space=pl.ANY)
BIAS = pltpu.VMEM((ROWS + HALF, HALF), F32)
TRI = pltpu.VMEM((HALF, HALF), F32)


def call(body, out, ins=None, outs=None, scratch=()):
    return pl.pallas_call(
        body,
        out_shape=out,
        **({} if ins is None else {"in_specs": ins}),
        out_specs=outs or jax.tree.map(lambda _: VM, out),
        scratch_shapes=scratch,
        cost_estimate=pl.CostEstimate(flops=1, bytes_accessed=1, transcendentals=0),
        compiler_params=pltpu.CompilerParams(vmem_limit_bytes=16 << 20),
    )


def in_hbm(x):
    return pltpu.with_memory_space_constraint(x, pltpu.HBM)


def pack(k_ref, v_ref, d_ref, o_ref, v_s, d_s, sem):
    copies = [
        pltpu.make_async_copy(v_ref, v_s, sem.at[0]),
        pltpu.make_async_copy(d_ref, d_s.at[0], sem.at[1]),
        pltpu.make_async_copy(k_ref, o_ref.at[0:ROWS, :], sem.at[2]),
    ]
    for c in copies:
        c.start()
    copies[1].wait()
    d = (d_s[...] + 1).astype(F32)
    rows = [d[:, a : a + DEPTH] for a in range(0, ROWS, DEPTH)]
    pad = jnp.zeros((SENT[0] - 2 * ROWS - 4, DEPTH), F32)
    o_ref[2 * ROWS :, :] = jnp.concatenate([*rows, pad], axis=0).astype(BF16)
    copies[0].wait()
    for a in range(0, ROWS, DEPTH):
        o_ref[ROWS + a : ROWS + a + DEPTH, :] = v_s[a : a + DEPTH, :].T
    copies[2].wait()


def hand(even_ref, odd_ref, after_ref, o_ref):
    core = lax.axis_index("ctx") % 2

    @pl.when(core == 0)
    def _():
        o_ref[...] = even_ref[0 : BLOCK[0], :]

    @pl.when(core == 1)
    def _():
        o_ref[...] = odd_ref[0 : BLOCK[0], :]


def keys(ref, half):
    return ref[half * HALF : (half + 1) * HALF, :]


def values(ref, half):
    at = ROWS + half * HALF
    return jnp.concatenate(
        [ref[at : at + DEPTH, :], ref[at + DEPTH : at + 2 * DEPTH, :]], axis=1
    )


def docs(ref, half):
    rows = ref[2 * ROWS : 2 * ROWS + 16, :].astype(F32)
    return jnp.concatenate(
        [rows[2 * half : 2 * half + 1, :], rows[2 * half + 1 : 2 * half + 2, :]], axis=1
    )


def column(row):
    return jnp.broadcast_to(row, (DEPTH, row.shape[1])).T


def widen(col, lanes):
    return jnp.concatenate([col] * (lanes // DEPTH), axis=1)


def first_doc(own_ref):
    return docs(own_ref, 0)[:, 0:1]


def row_mask(own_ref):
    both = jnp.concatenate([docs(own_ref, 0), docs(own_ref, 1)], axis=1)
    return jnp.where(both == first_doc(own_ref), 1.0, 0.0)


def row_bias(own_ref):
    return (1.0 - row_mask(own_ref)) * NEG


def key_match(own_ref, ref, half):
    return jnp.where(docs(ref, half) == first_doc(own_ref), 1.0, 0.0)


def key_bias(own_ref, ref, half):
    return column((1.0 - key_match(own_ref, ref, half)) * NEG)


def dot(a, b):
    return jnp.dot(a, b, preferred_element_type=F32)


def fold(e):
    return jnp.sum(e.reshape(e.shape[0] // 8, 8, e.shape[1]), axis=0)


def all_keys(ref):
    return ref[0:ROWS, :]


def all_values(ref):
    return jnp.concatenate([values(ref, 0), values(ref, 1)], axis=1)


def head(h):
    return slice(h * DEPTH, (h + 1) * DEPTH)


def eight(h):
    return slice(h * 8, (h + 1) * 8)


def staged(units, first, rest, depth=1):
    held = [first(u) for u in units[:depth]]
    for i, u in enumerate(units):
        if i + depth < len(units):
            held.append(first(units[i + depth]))
        rest(u, held.pop(0))


def triangle(strict):
    key = lax.broadcasted_iota(jnp.int32, (HALF, HALF), 0)
    row = lax.broadcasted_iota(jnp.int32, (HALF, HALF), 1)
    keep = key > row if strict else key <= row
    return jnp.where(keep, 0.0, NEG)


def beside_keys(own_ref, ref):
    both = jnp.concatenate([key_match(own_ref, ref, k) for k in range(2)], axis=1)
    at = lax.broadcasted_iota(jnp.int32, (DEPTH, ROWS), 0)
    rows = jnp.where(at < 64, (1.0 - both) * NEG, 1.0)
    return rows.astype(BF16).T


def below_queries(own_ref):
    at = lax.broadcasted_iota(jnp.int32, (DEPTH, ROWS), 0)
    row = jnp.where(at == 64, row_bias(own_ref), 0.0)
    return jnp.where(at == 0, 1.0, row).astype(BF16)


def full_heads(own_ref, refs, qt_ref, acc_in, sum_in, put, depth):
    cat = lambda parts, axis: jnp.concatenate(parts, axis=axis)
    kk = cat([cat([all_keys(x), beside_keys(own_ref, x)], 1) for x in refs], 0)
    vv = cat([all_values(x) for x in refs], 1)
    below = below_queries(own_ref)

    def blocks(h):
        return ROWS * (len(refs) if h >= SOLO else 1)

    def first(h):
        return dot(kk[: blocks(h), :], cat([qt_ref[head(h), :], below], 0))

    def rest(h, s):
        e = jnp.exp2(s * SCALE)
        o = dot(vv[:, : blocks(h)], e.astype(BF16))
        put(h, acc_in[head(h), :] + o, sum_in[eight(h), :] + fold(e))

    staged(range(HEADS), first, rest, depth)


def cut_heads(qt_ref, b_ref, kk, vv, cut, put):
    def first(u):
        h, r = u
        return dot(kk[r], qt_ref[head(h), r * HALF : (r + 1) * HALF])

    def rest(u, s):
        h, r = u
        e = jnp.exp2(s * SCALE + b_ref[cut[r], :])
        put(h, slice(r * HALF, (r + 1) * HALF), dot(vv[r], e.astype(BF16)), fold(e))

    staged([(h, r) for h in range(HEADS) for r in range(2)], first, rest, 2)


def own_block(q_ref, own_ref, qt_ref, acc_ref, sum_ref, b_ref, q_s, sem):
    copies = [
        pltpu.make_async_copy(q_ref.at[:, head(h)], q_s.at[:, head(h)], sem.at[h])
        for h in range(HEADS)
    ]
    for c in copies:
        c.start()
    rows = [docs(own_ref, 0), docs(own_ref, 1)]
    cols = [widen(column(r), HALF) for r in rows]
    apart = lambda k, r: jnp.where(cols[k] == rows[r], 0.0, NEG)
    tri = triangle(False)
    b_ref[0:HALF, :] = apart(0, 1)
    b_ref[HALF:ROWS, :] = apart(1, 1) + tri
    b_ref[ROWS : ROWS + HALF, :] = apart(0, 0) + tri
    for h in range(HEADS):
        copies[h].wait()
        qt_ref[head(h), :] = q_s[:, head(h)].T

    def put(h, cs, o, t):
        acc_ref[head(h), cs] = o
        sum_ref[eight(h), cs] = t

    cut_heads(
        qt_ref,
        b_ref,
        (keys(own_ref, 0), all_keys(own_ref)),
        (values(own_ref, 0), all_values(own_ref)),
        (slice(ROWS, ROWS + HALF), slice(0, ROWS)),
        put,
    )


def full_block(own_ref, ref, qt_ref, acc_in, sum_in, acc_ref, sum_ref):
    def put(h, acc, sums):
        acc_ref[head(h), :] = acc
        sum_ref[eight(h), :] = sums

    full_heads(own_ref, (ref,), qt_ref, acc_in, sum_in, put, 1)


def solo_block(own_ref, ref, qt_ref, acc_in, sum_in, acc_ref, sum_ref):
    kk = jnp.concatenate([all_keys(ref), beside_keys(own_ref, ref)], axis=1)
    vv = all_values(ref)
    below = below_queries(own_ref)

    def first(h):
        return dot(kk, jnp.concatenate([qt_ref[head(h), :], below], axis=0))

    def rest(h, s):
        e = jnp.exp2(s * SCALE)
        acc_ref[head(h), :] = acc_in[head(h), :] + dot(vv, e.astype(BF16))
        sum_ref[eight(h), :] = sum_in[eight(h), :] + fold(e)

    staged(range(SOLO), first, rest, 1)
    acc_ref[SOLO * DEPTH :, :] = acc_in[SOLO * DEPTH :, :]
    sum_ref[SOLO * 8 :, :] = sum_in[SOLO * 8 :, :]


def far_block(own_ref, ref, qt_ref, acc_in, sum_in, acc_ref, sum_ref, b_ref):
    left, right = slice(0, HALF), slice(HALF, ROWS)

    b_ref[...] = triangle(True)
    beside = beside_keys(own_ref, ref)
    k0 = jnp.concatenate([keys(ref, 0), beside[left, :]], axis=1)
    k1 = jnp.concatenate([keys(ref, 1), beside[right, :]], axis=1)
    below = below_queries(own_ref)

    def first(h):
        q = jnp.concatenate([qt_ref[head(h), :], below], axis=0)
        return dot(k0, q[:, left]), dot(k1, q)

    def rest(h, s):
        s0, s1 = s
        tri = b_ref[...]
        e0 = jnp.exp2(s0 * SCALE + tri)
        cut = jnp.concatenate([s1[:, left] * SCALE, s1[:, right] * SCALE + tri], axis=1)
        e1 = jnp.exp2(cut)
        o1, t1 = dot(values(ref, 1), e1.astype(BF16)), fold(e1)
        o0 = dot(values(ref, 0), e0.astype(BF16)) + o1[:, left]
        t0 = fold(e0) + t1[:, left]
        acc_ref[head(h), left] = acc_in[head(h), left] + o0
        acc_ref[head(h), right] = acc_in[head(h), right] + o1[:, right]
        sum_ref[eight(h), left] = sum_in[eight(h), left] + t0
        sum_ref[eight(h), right] = sum_in[eight(h), right] + t1[:, right]

    staged(range(HEADS), first, rest, 2)


def careful(own_ref, full_refs, far_ref, qt_ref, out_ref, s_ref):
    refs = (own_ref, *full_refs, far_ref)
    lanes = 128
    key0 = lax.broadcasted_iota(jnp.int32, (HALF, lanes), 0)
    row0 = lax.broadcasted_iota(jnp.int32, (HALF, lanes), 1)
    mask = row_mask(own_ref)

    def one(step, carry):
        h, c = step // 4, step % 4
        hs = pl.ds(pl.multiple_of(h * DEPTH, DEPTH), DEPTH)
        cs = pl.ds(pl.multiple_of(c * lanes, lanes), lanes)
        qt = qt_ref[hs, cs]
        row = row0 + c * lanes
        both = [docs(own_ref, r // 2)[:, r % 2 * 128 : r % 2 * 128 + 128] for r in range(4)]
        own_row = mrow = None
        for r in range(4):
            picked = jnp.where(c == r, both[r], 0.0)
            m = jnp.where(c == r, mask[:, r * 128 : (r + 1) * 128], 0.0)
            own_row = picked if own_row is None else own_row + picked
            mrow = m if mrow is None else mrow + m
        for n, ref in enumerate(refs):
            for k in range(2):
                key = key0 + k * HALF
                col = column(docs(ref, k))
                if n == 0:
                    keep = (col == own_row) & (key <= row)
                else:
                    keep = (column(key_match(own_ref, ref, k)) * mrow) > 0.5
                    if ref is far_ref:
                        keep = keep & (key > row)
                s = dot(keys(ref, k), qt) * SCALE
                at = (2 * n + k) * HALF
                s_ref[at : at + HALF, :] = jnp.where(keep, s, NEG)
        top = jnp.max(s_ref[...], axis=0, keepdims=True)
        o, t = jnp.zeros((DEPTH, lanes), F32), jnp.zeros((1, lanes), F32)
        for n, ref in enumerate(refs):
            for k in range(2):
                at = (2 * n + k) * HALF
                e = jnp.exp2(s_ref[at : at + HALF, :] - top)
                t = t + jnp.sum(e, axis=0, keepdims=True)
                o = o + dot(values(ref, k), e.astype(BF16))
        out_ref[cs, hs] = (o / t).T.astype(BF16)
        return carry

    lax.fori_loop(0, HEADS * 4, one, 0)


def last_block(
    own_ref, pa_ref, pb_ref, e1_ref, e2_ref, qt_ref, acc_in, sum_in,
    out_ref, o_s, s_ref, good_ref, sem,
):
    copies = [
        pltpu.make_async_copy(o_s.at[rows, :], out_ref.at[rows, :], sem.at[n])
        for n, rows in enumerate(slice(a, a + 128) for a in range(0, ROWS, 128))
    ]

    def put(h, acc, sums):
        t = jnp.sum(sums, axis=0, keepdims=True)
        good_ref[h : h + 1, :] = jnp.where((t > LOW) & (t < HIGH), 1.0, 0.0)
        o_s[:, head(h)] = (acc * (1.0 / t)).astype(BF16).T

    full_heads(own_ref, (e2_ref, pa_ref), qt_ref, acc_in, sum_in, put, 2)
    for c in copies:
        c.start()
    bad = jnp.min(good_ref[...]) < 0.5
    for c in copies:
        c.wait()

    @pl.when(bad)
    def _():
        careful(own_ref, (pa_ref, e1_ref, e2_ref), pb_ref, qt_ref, o_s, s_ref)
        for c in copies:
            c.start()
        for c in copies:
            c.wait()


def local(queries, k, v, doc_ids):
    size = lax.axis_size("ctx")
    block = jax.ShapeDtypeStruct(BLOCK, BF16)
    qt_out = jax.ShapeDtypeStruct(QT, BF16)
    acc_out = jax.ShapeDtypeStruct(QT, F32)
    sum_out = jax.ShapeDtypeStruct(SUMS, F32)
    dma = pltpu.SemaphoreType.DMA

    def move(x, pairs):
        return lax.ppermute(x, "ctx", [(a, b) for a, b in pairs if 0 <= b < size])

    own = call(
        pack,
        jax.ShapeDtypeStruct(SENT, BF16),
        (ANY, ANY, ANY),
        scratch=(
            pltpu.VMEM((ROWS, DEPTH), BF16),
            pltpu.VMEM((1, ROWS), jnp.int32),
            dma((3,)),
        ),
    )(in_hbm(k), in_hbm(v), in_hbm(doc_ids))
    pa = move(own, [(i, i + (1 if i % 2 else 3)) for i in range(size)])
    pb = move(own, [(i, i + 4) for i in range(size)])
    qt, acc, sums = call(
        own_block,
        (qt_out, acc_out, sum_out),
        (ANY, VM),
        scratch=(BIAS, pltpu.VMEM((ROWS, HEADS * DEPTH), BF16), dma((HEADS,))),
    )(in_hbm(queries), own)
    swap = [(i, i ^ 1) for i in range(size)]
    hand_over = call(hand, block, (VM, VM, ANY))
    full = call(full_block, (acc_out, sum_out))
    e1 = move(hand_over(own, pb, sums), swap)
    acc, sums = call(far_block, (acc_out, sum_out), scratch=(TRI,))(
        own, pb, qt, acc, sums
    )
    acc, sums = full(own, e1, qt, acc, sums)
    e2 = move(hand_over(pa, pa, sums), swap)
    acc, sums = call(solo_block, (acc_out, sum_out))(own, pa, qt, acc, sums)
    return call(
        last_block,
        jax.ShapeDtypeStruct(queries.shape, BF16),
        outs=ANY,
        scratch=(
            pltpu.VMEM((ROWS, HEADS * DEPTH), BF16),
            pltpu.VMEM((10 * HALF, 128), F32),
            pltpu.VMEM((HEADS, ROWS), F32),
            dma((4,)),
        ),
    )(own, pa, pb, e1, e2, qt, acc, sums)


def solution(mesh):
    return jax.shard_map(
        local,
        mesh=mesh,
        in_specs=(P("ctx", None), P("ctx", None), P("ctx", None), P("ctx")),
        out_specs=P("ctx", None),
        check_vma=False,
    )
```
